512 devices in a mesh: leaf: 512 (over y, z, x, core).
Axes of the slice: x: 4, y: 4, z: 16, core: 2. Of those that a mesh axis runs over, the one named last changes fastest.
Arguments:
- sources: float32 [16, 1048576], P(None, 'leaf'), may hold values from -6 to 6
- leaf_cluster_basis: float32 [8192, 64, 128], P('leaf'), may hold values from -0.5 to 0.5
- local_transfer: float32 [15360, 4096], P('leaf'), may hold values from -0.5 to 0.5
- far_coupling: float32 [15360, 3, 4096], P('leaf'), may hold values from -0.5 to 0.5
- far_partner: int32 [15360, 3], P('leaf'), may hold values from 0 to 8191, as said below
- far_count: int32 [15360], P('leaf'), may hold values from 1 to 3
- top_transfer: float32 [512, 9, 4096], P('leaf'), may hold values from -0.5 to 0.5
- top_coupling: float32 [512, 9, 2, 4096], P('leaf'), may hold values from -0.75 to 0.75
- near_block: float32 [8192, 2, 128, 128], P('leaf'), may hold values from -0.375 to 0.375
- near_partner: int32 [8192, 2], P('leaf'), may hold values from 0 to 8191, as said below
- near_count: int32 [8192], P('leaf'), may hold values from 1 to 2
Outputs:
- product: float32 [16, 1048576], P(None, 'leaf')
The draws below stay inside these ranges and needn't reach their ends.
Inputs may be any that keep to these rules, and one draw needn't show every extreme that they name: Each entry of far_partner is the index, within the same level, of a cluster 1 to n positions away from the row's own cluster, n being the clusters of that level on one device (numbering as in the reference program). `near_partner`: slot 0 of each row is the row's own leaf; every other entry is a leaf 1 to 8 positions away from it.
All inputs are finite; a program needn't handle non-finite values.
Results may differ from the reference program's by a relative error of at most 0.0003.
Values sent between devices are 32-bit elements; how exact they have to be, the bound alone decides.
No kernel may reach another device: no remote copies, remote signals or barrier semaphores. Data moves between devices by JAX's collectives and lax.ppermute only.
A program may use at most 64 MiB of HBM per device.

```python
import jax
import jax.numpy as jnp
import numpy as np
from jax import lax

LEAF = 128
BASIS_ORDER = 64
RIGHT_COLUMNS = 16
LEVELS_LOCAL = 4
MAXP = 3
NEARP = 2
LEAVES_PER_UNIT = 16
LOCAL = 30
NEAR_REACH = 8
TOPLEV = 9
TOTAL_LEAVES = 8192
CLUSTERS = 15360
NPTS = 1048576
N_LEAF = 512


def level_tables():
    sizes_list = []
    offsets_list = []
    offset = 0
    for level in range(LEVELS_LOCAL):
        per_device = LEAVES_PER_UNIT >> level
        sizes_list += [per_device] * per_device
        offsets_list += [offset] * per_device
        offset += per_device
    return (np.array(sizes_list, np.int32), np.array(offsets_list, np.int32))


def draw_far_partner(key, part):
    key = jax.random.fold_in(key, 11)
    sizes_table, offsets_table = level_tables()
    row_index = jnp.arange(CLUSTERS, dtype=jnp.int32)
    device = row_index // LOCAL
    inside = row_index % LOCAL
    per_device = jnp.asarray(sizes_table)[inside]
    offset = jnp.asarray(offsets_table)[inside]
    own_index = device * per_device + inside - offset
    key_distance, key_direction = jax.random.split(key)
    raw = jax.random.randint(key_distance, (CLUSTERS, MAXP), 0, 1 << 20)
    distance = 1 + raw % per_device[:, None]
    direction = 2 * jax.random.randint(key_direction, (CLUSTERS, MAXP), 0, 2) - 1
    candidate = own_index[:, None] + direction * distance
    limit = per_device[:, None] * N_LEAF
    outside = (candidate < 0) | (candidate >= limit)
    return jnp.where(outside, own_index[:, None] - direction * distance, candidate).astype(jnp.int32)


def draw_far_count(key, part):
    key = jax.random.fold_in(key, 12)
    key_values, key_pick = jax.random.split(key)
    values = jax.random.randint(key_values, (CLUSTERS,), 1, MAXP + 1)
    chosen = jax.random.randint(key_pick, (), 0, CLUSTERS)
    return jnp.where(jnp.arange(CLUSTERS) == chosen, MAXP, values).astype(jnp.int32)


def draw_near_partner(key, part):
    key = jax.random.fold_in(key, 13)
    own_index = jnp.arange(TOTAL_LEAVES, dtype=jnp.int32)
    position = own_index % LEAVES_PER_UNIT
    first_leaf = (position == 0)[:, None]
    last_leaf = (position == LEAVES_PER_UNIT - 1)[:, None]
    leading = (jnp.arange(NEARP - 1) == 0)[None, :]
    key_distance, key_direction = jax.random.split(key)
    distance = jax.random.randint(key_distance, (TOTAL_LEAVES, NEARP - 1), 1, NEAR_REACH + 1)
    direction = 2 * jax.random.randint(key_direction, (TOTAL_LEAVES, NEARP - 1), 0, 2) - 1
    edge = leading & (first_leaf | last_leaf)
    distance = jnp.where(edge, NEAR_REACH, distance)
    direction = jnp.where(leading & first_leaf, -1, jnp.where(leading & last_leaf, 1, direction))
    candidate = own_index[:, None] + direction * distance
    outside = (candidate < 0) | (candidate >= TOTAL_LEAVES)
    others = jnp.where(outside, own_index[:, None] - direction * distance, candidate)
    return jnp.concatenate([own_index[:, None], others], axis=1).astype(jnp.int32)


def draw_near_count(key, part):
    key = jax.random.fold_in(key, 14)
    values = jax.random.randint(key, (TOTAL_LEAVES,), 1, NEARP + 1)
    position = jnp.arange(TOTAL_LEAVES, dtype=jnp.int32) % LEAVES_PER_UNIT
    edge = (position == 0) | (position == LEAVES_PER_UNIT - 1)
    return jnp.where(edge, NEARP, values).astype(jnp.int32)


def levels(key, extent, pieces, low, top_value):
    gain = 1.0
    for dim, shards_of in pieces:
        draws = jax.random.uniform(jax.random.fold_in(jax.random.fold_in(key, 6), dim), (shards_of,), jnp.float32, low / len(pieces), top_value / len(pieces))
        gain = gain * jnp.repeat(jnp.exp(draws), extent[dim] // shards_of).reshape((-1,) + (1,) * (len(extent) - 1 - dim))
    return gain


def bell_draw(own_key, dims, width, reach, cuts=(), held_as=jnp.bfloat16):
    values = jax.random.normal(own_key, dims, jnp.float32) * width
    if len(cuts) > 0:
        values = levels(own_key, dims, cuts, -0.22, 0.18) * values
    return jnp.clip(values, min=-reach, max=reach).astype(held_as)


def setup_inputs(seed: int = 0) -> dict:
    splits = jax.random.split(jax.random.key(seed), 12)
    sources = bell_draw(splits[0], (RIGHT_COLUMNS, NPTS), 1.0, 6.0, ((1, 512),), jnp.float32)
    leaf_cluster_basis = bell_draw(splits[1], (TOTAL_LEAVES, BASIS_ORDER, LEAF), LEAF ** -0.5, 0.5, ((0, 512),), jnp.float32)
    local_transfer = bell_draw(splits[2], (CLUSTERS, BASIS_ORDER * BASIS_ORDER), (2 * BASIS_ORDER) ** -0.5, 0.5, ((0, 512),), jnp.float32)
    far_coupling = bell_draw(splits[3], (CLUSTERS, MAXP, BASIS_ORDER * BASIS_ORDER), (2 * BASIS_ORDER) ** -0.5, 0.5, ((0, 512),), jnp.float32)
    far_partner = draw_far_partner(jax.random.fold_in(splits[11], 71), 0)
    far_count = draw_far_count(jax.random.fold_in(splits[11], 71), 0)
    top_transfer = bell_draw(splits[6], (N_LEAF, TOPLEV, BASIS_ORDER * BASIS_ORDER), (2 * BASIS_ORDER) ** -0.5, 0.5, ((0, 512),), jnp.float32)
    top_coupling = bell_draw(splits[7], (N_LEAF, TOPLEV, 2, BASIS_ORDER * BASIS_ORDER), BASIS_ORDER ** -0.5, 0.75, ((0, 512),), jnp.float32)
    near_block = bell_draw(splits[8], (TOTAL_LEAVES, NEARP, LEAF, LEAF), (2 * LEAF) ** -0.5, 0.375, ((0, 512),), jnp.float32)
    near_partner = draw_near_partner(jax.random.fold_in(splits[11], 71), 0)
    near_count = draw_near_count(jax.random.fold_in(splits[11], 71), 0)
    return dict(sources=sources, leaf_cluster_basis=leaf_cluster_basis, local_transfer=local_transfer, far_coupling=far_coupling, far_partner=far_partner, far_count=far_count, top_transfer=top_transfer, top_coupling=top_coupling, near_block=near_block, near_partner=near_partner, near_count=near_count)


HIGH_ACCURACY = lax.Precision.HIGHEST


def level_layout():
    result = []
    offset = 0
    for level in range(LEVELS_LOCAL):
        clusters = LEAVES_PER_UNIT >> level
        result.append((clusters, offset))
        offset += clusters
    return result


def reference(sources, leaf_cluster_basis, local_transfer, far_coupling, far_partner, far_count, top_transfer, top_coupling, near_block, near_partner, near_count):
    device_list = N_LEAF
    leaf_entries = sources.reshape(RIGHT_COLUMNS, TOTAL_LEAVES, LEAF)
    present_value = jnp.einsum('ztq,tfq->tzf', leaf_entries, leaf_cluster_basis, precision=HIGH_ACCURACY).reshape(device_list, LEAVES_PER_UNIT, RIGHT_COLUMNS, BASIS_ORDER)
    transfers = local_transfer.reshape(device_list, LOCAL, BASIS_ORDER, BASIS_ORDER)
    couplings = far_coupling.reshape(device_list, LOCAL, MAXP, BASIS_ORDER, BASIS_ORDER)
    partners = far_partner.reshape(device_list, LOCAL, MAXP)
    counts = far_count.reshape(device_list, LOCAL)
    layout = level_layout()
    coefficients = []
    for clusters, offset in layout:
        coefficients.append(present_value)
        carried = jnp.einsum('dnsr,dnrq->dnsq', present_value, transfers[:, offset:offset + clusters], precision=HIGH_ACCURACY)
        present_value = carried.reshape(device_list, clusters // 2, 2, RIGHT_COLUMNS, BASIS_ORDER).sum(axis=2)
    far_terms = []
    for (clusters, offset), coefs in zip(layout, coefficients):
        flattened = coefs.reshape(device_list * clusters, RIGHT_COLUMNS, BASIS_ORDER)
        picked = flattened[partners[:, offset:offset + clusters]]
        present = (jnp.arange(MAXP)[None, None, :] < counts[:, offset:offset + clusters, None]).astype(jnp.float32)
        far_terms.append(jnp.einsum('dnpsr,dnprq->dnsq', picked * present[..., None, None], couplings[:, offset:offset + clusters], precision=HIGH_ACCURACY))
    levels_top = device_list.bit_length() - 1
    top_steps = top_transfer.reshape(device_list, levels_top, BASIS_ORDER, BASIS_ORDER)
    siblings = top_coupling.reshape(device_list, levels_top, 2, BASIS_ORDER, BASIS_ORDER)
    below = present_value[:, 0]
    stored = []
    for level in range(1, levels_top + 1):
        firsts = jnp.arange(device_list >> (level - 1)) * (2 ** (level - 1))
        owners = jnp.arange(device_list >> level) * (2 ** level)
        below_steps = top_steps[firsts, level - 1]
        carried = jnp.einsum('gsr,grq->gsq', below, below_steps, precision=HIGH_ACCURACY)
        parent = carried[0::2] + carried[1::2]
        to_left = jnp.einsum('gsr,grq->gsq', below[1::2], siblings[owners, level - 1, 0], precision=HIGH_ACCURACY)
        to_right = jnp.einsum('gsr,grq->gsq', below[0::2], siblings[owners, level - 1, 1], precision=HIGH_ACCURACY)
        stored.append((below_steps, jnp.stack([to_left, to_right], axis=1).reshape(-1, RIGHT_COLUMNS, BASIS_ORDER)))
        below = parent
    downward = jnp.zeros((1, RIGHT_COLUMNS, BASIS_ORDER), jnp.float32)
    for steps_here, coupled in reversed(stored):
        spread = jnp.repeat(downward, 2, axis=0)
        downward = jnp.einsum('gsq,grq->gsr', spread, steps_here, precision=HIGH_ACCURACY) + coupled
    present_value = downward[:, None]
    for (clusters, offset), coupled in reversed(list(zip(layout, far_terms))):
        spread = jnp.repeat(present_value, 2, axis=1)
        present_value = jnp.einsum('dnsq,dnrq->dnsr', spread, transfers[:, offset:offset + clusters], precision=HIGH_ACCURACY) + coupled
    distant_field = jnp.einsum('pvx,pxb->vpb', present_value.reshape(TOTAL_LEAVES, RIGHT_COLUMNS, BASIS_ORDER), leaf_cluster_basis, precision=HIGH_ACCURACY)
    picked = leaf_entries[:, near_partner]
    present = (jnp.arange(NEARP)[None, :] < near_count[:, None]).astype(jnp.float32)
    near_field = jnp.einsum('lpkj,slpj->slk', near_block, picked * present[None, :, :, None], precision=HIGH_ACCURACY)
    return (distant_field + near_field).reshape(RIGHT_COLUMNS, NPTS)
```

```python
import jax
import jax.numpy as jnp
from jax import lax
from jax.experimental import pallas as pl
from jax.experimental.pallas import tpu as pltpu
from jax.sharding import PartitionSpec as P

F32 = jnp.float32
BF16 = jnp.bfloat16
RANK = 64
LEAVES = 16
POINTS = 128
LOCAL = 30
SLOTS = 3
NEAR = 2
REACH = 8
GROUP_BITS = 4
TOP_BITS = 9
GROUP = 1 << GROUP_BITS
GROUPS = 1 << (TOP_BITS - GROUP_BITS)
LAYOUT = ((16, 0), (8, 16), (4, 24), (2, 28))
VMEM_BYTES = 48 * 1024 * 1024


def split(x):
    high = x.astype(BF16)
    return high, (x - high.astype(F32)).astype(BF16)


def lanes(rows):
    return lax.broadcasted_iota(jnp.int32, (rows, 128), 1)


def table_form(table):
    high, low = split(table)
    return jnp.concatenate([high, low, high, low], axis=0)


def coef_form(packed):
    lane = lanes(8)
    even = 2 * (lane % 32)
    parts = [
        jnp.take_along_axis(packed, even + shift, axis=1) for shift in (0, 64, 1, 65)
    ]
    full = jnp.concatenate(parts, axis=0)
    high, low = split(full)
    return jnp.where(lanes(32) < 64, high.astype(F32), low.astype(F32)).astype(BF16)


def dot(a, b):
    return lax.dot_general(a, b, (((1,), (0,)), ((), ())), preferred_element_type=F32)


def dot_t(a, b):
    return lax.dot_general(a, b, (((1,), (1,)), ((), ())), preferred_element_type=F32)


def fold(out):
    left = lanes(8) < 64
    straight = jnp.where(left, out[0:8], out[24:32])
    crossed = jnp.where(left, out[8:16], out[16:24])
    return straight + pltpu.roll(crossed, 64, 1)


def times(packed, table):
    return fold(dot(coef_form(packed), table_form(table)))


def row_form(packed):
    left = lanes(8) < 64
    turned = pltpu.roll(packed, 64, 1)
    zero = jnp.zeros_like(packed)
    full = jnp.concatenate(
        [
            jnp.where(left, packed, zero),
            jnp.where(left, turned, zero),
            jnp.where(left, zero, turned),
            jnp.where(left, zero, packed),
        ],
        axis=0,
    )
    return split(full)


def weave(even_odd):
    lane = lanes(8)
    place = (lane % 64) // 2
    wide = jnp.concatenate([even_odd] * 4, axis=1)
    pick = [jnp.take_along_axis(wide[8 * k : 8 * k + 8], place, axis=1) for k in range(4)]
    even = lane % 2 == 0
    return jnp.where(
        lane < 64, jnp.where(even, pick[0], pick[2]), jnp.where(even, pick[1], pick[3])
    )


def times_t_raw(rows, high, low):
    row_high, row_low = rows
    both = dot_t(jnp.concatenate([row_high, row_low], axis=0), high)
    return both[:32] + both[32:] + dot_t(row_high, low)


def times_t(packed, table):
    high, low = split(table)
    return weave(times_t_raw(row_form(packed), high, low))


def unpack(packed):
    return jnp.concatenate([packed[:, :RANK], packed[:, RANK:]], axis=0)


def pack(value):
    return jnp.concatenate([value[:8], value[8:]], axis=1)


def up_kernel(sources, basis, transfer, coefs, root, tables):
    table = transfer[...].reshape(LOCAL, 32, 128)
    for row in range(LOCAL):
        high, low = split(table[row])
        tables[row, 0:32] = high
        tables[row, 32:64] = low
    for leaf in range(LEAVES):
        high, low = split(sources[:, leaf * POINTS : (leaf + 1) * POINTS])
        basis_high, basis_low = split(basis[leaf])
        both = dot_t(jnp.concatenate([high, low], axis=0), basis_high)
        coefs[leaf] = pack(both[:16] + both[16:] + dot_t(high, basis_low))
    for level, (clusters, offset) in enumerate(LAYOUT):
        for parent in range(clusters // 2):
            first = offset + 2 * parent
            left = jnp.concatenate(
                [coef_form(coefs[first]), coef_form(coefs[first + 1])], axis=1
            )
            halves = [tables[first], tables[first], tables[first + 1], tables[first + 1]]
            value = fold(dot(left, jnp.concatenate(halves, axis=0)))
            if clusters > 2:
                coefs[offset + clusters + parent] = value
            else:
                root[...] = value


def near_kernel(partner, count, device, own, low, high, block, out, leaves):
    for leaf in range(LEAVES):
        leaves[REACH + leaf] = own[:, leaf * POINTS : (leaf + 1) * POINTS]
    for leaf in range(REACH):
        leaves[leaf] = low[:, leaf * POINTS : (leaf + 1) * POINTS]
        leaves[REACH + LEAVES + leaf] = high[:, leaf * POINTS : (leaf + 1) * POINTS]
    first = device[0] * LEAVES - REACH
    for leaf in range(LEAVES):
        total = None
        for slot in range(NEAR):
            place = jnp.clip(partner[leaf, slot] - first, 0, LEAVES + 2 * REACH - 1)
            used = (slot < count[leaf]).astype(F32)
            picked_high, picked_low = split(leaves[place] * used)
            block_high, block_low = split(block[leaf, slot])
            both = dot_t(jnp.concatenate([picked_high, picked_low], axis=0), block_high)
            value = both[:16] + both[16:] + dot_t(picked_high, block_low)
            total = value if total is None else total + value
        out[:, leaf * POINTS : (leaf + 1) * POINTS] = total


def far_kernel(partner, count, device, own, low, high, coupling, out, extended):
    extended[0:LOCAL] = low[...]
    extended[LOCAL : 2 * LOCAL] = own[...]
    extended[2 * LOCAL : 3 * LOCAL] = high[...]
    tables = [coupling[slot].reshape(LOCAL, 32, 128) for slot in range(SLOTS)]
    for clusters, offset in LAYOUT:
        for cluster in range(clusters):
            row = offset + cluster
            left = []
            right = []
            for slot in range(SLOTS):
                index = partner[row, slot]
                side = jnp.clip(index // clusters - device[0] + 1, 0, 2)
                place = side * LOCAL + offset + index % clusters
                used = (slot < count[row]).astype(F32)
                left.append(coef_form(extended[place] * used))
                right.append(table_form(tables[slot][row]))
            out[row] = fold(dot(jnp.concatenate(left, axis=1), jnp.concatenate(right, axis=0)))


def share_kernel(member, root, own, table, blocks, chain):
    value = root[...]
    chain[0] = value
    for level in range(GROUP_BITS):
        value = times(value, own[...] if level == 0 else table[level - 1])
        if level + 1 < GROUP_BITS:
            chain[level + 1] = value
    for other in range(GROUP):
        apart = member[0] ^ other
        level = sum((apart >= (1 << bit)).astype(jnp.int32) for bit in range(1, GROUP_BITS))
        blocks[other, 0:8] = chain[level]
        blocks[other, 8:16] = value


def rise_kernel(position, arrived, own, table, sibling, blocks, chain):
    member = position[0]
    for level in range(GROUP_BITS):
        total = None
        for apart in range(1 << level, 2 << level):
            value = arrived[member ^ apart, 0:8]
            total = value if total is None else total + value
        sibling[level] = total
    value = arrived[0, 8:16]
    for other in range(1, GROUP):
        value = value + arrived[other, 8:16]
    steps = TOP_BITS - GROUP_BITS
    chain[0] = value
    for level in range(steps - 1):
        value = times(value, own[...] if level == 0 else table[level - 1])
        chain[level + 1] = value
    for other in range(GROUPS):
        apart = position[1] ^ other
        level = sum((apart >= (1 << bit)).astype(jnp.int32) for bit in range(1, steps))
        blocks[other] = chain[level]


def turn_kernel(position, arrived, own, table, out):
    steps = TOP_BITS - GROUP_BITS
    group = position[1]
    value = None
    terms = []
    for level in range(steps):
        total = None
        for apart in range(1 << level, 2 << level):
            piece = arrived[group ^ apart]
            total = piece if total is None else total + piece
        terms.append(times(total, table[steps - 2 + steps - 1 - level]))
    value = terms[steps - 1]
    for level in range(steps - 2, -1, -1):
        value = times_t(value, own[...] if level == 0 else table[level - 1]) + terms[level]
    for other in range(GROUP):
        out[other] = value


def down_kernel(arrived, sibling, own, table, tables, far, basis, near, out, fields):
    value = arrived[0]
    terms = [
        times(sibling[level], table[GROUP_BITS - 1 + GROUP_BITS - 1 - level])
        for level in range(GROUP_BITS)
    ]
    for level in range(GROUP_BITS - 1, -1, -1):
        value = times_t(value, own[...] if level == 0 else table[level - 1]) + terms[level]
    parents = [value]
    for clusters, offset in reversed(LAYOUT):
        following = []
        for parent in range(clusters // 2):
            first = offset + 2 * parent
            high = jnp.concatenate([tables[first, 0:32], tables[first + 1, 0:32]], axis=0)
            low = jnp.concatenate([tables[first, 32:64], tables[first + 1, 32:64]], axis=0)
            raw = times_t_raw(row_form(parents[parent]), high, low)
            following.append(weave(raw[:, 0:32]) + far[first])
            following.append(weave(raw[:, 32:64]) + far[first + 1])
        parents = following
    for leaf in range(LEAVES):
        high, low = split(unpack(parents[leaf]))
        basis_high, basis_low = split(basis[leaf])
        both = dot(jnp.concatenate([high, low], axis=0), basis_high)
        place = slice(leaf * POINTS, (leaf + 1) * POINTS)
        out[:, place] = both[:16] + both[16:] + dot(high, basis_low) + near[:, place]


def call(kernel, name, outs, args, scalars=0, scratch=()):
    vmem = pl.BlockSpec(memory_space=pltpu.VMEM)
    smem = pl.BlockSpec(memory_space=pltpu.SMEM)
    single = not isinstance(outs, list)
    result = pl.pallas_call(
        kernel,
        out_shape=outs,
        in_specs=[smem] * scalars + [vmem] * (len(args) - scalars),
        out_specs=vmem if single else [vmem] * len(outs),
        scratch_shapes=list(scratch),
        compiler_params=pltpu.CompilerParams(vmem_limit_bytes=VMEM_BYTES),
        name=name,
    )(*args)
    return result


def shape(*dims, dtype=F32):
    return jax.ShapeDtypeStruct(dims, dtype)


def permute(value, pairs):
    return lax.ppermute(value, "leaf", pairs)


def hand_down(table, other, device, bit, low, high):
    count = lax.axis_size("leaf")
    pairs = [(i, i + (1 << bit)) for i in range(0, count, 2 << bit)]
    payload = jnp.concatenate([table[low : high - 1], other[None]], axis=0)
    arrived = permute(payload, pairs)
    right = (device >> bit) & 1 == 1
    merged = jnp.where(right, arrived, table[low:high])
    return jnp.concatenate([table[:low], merged, table[high:]], axis=0)


def on_device(
    sources,
    leaf_cluster_basis,
    local_transfer,
    far_coupling,
    far_partner,
    far_count,
    top_transfer,
    top_coupling,
    near_block,
    near_partner,
    near_count,
):
    count = lax.axis_size("leaf")
    device = lax.axis_index("leaf").astype(jnp.int32)
    member = device % GROUP
    group = device // GROUP
    index = device.reshape(1)
    position = jnp.stack([member, group])
    forward = [(i, i + 1) for i in range(count - 1)]
    backward = [(i + 1, i) for i in range(count - 1)]

    reach = REACH * POINTS
    source_low = permute(sources[:, -reach:], forward)
    source_high = permute(sources[:, :reach], backward)

    transfers = top_transfer.reshape(TOP_BITS, 32, 128)
    couplings = top_coupling.reshape(TOP_BITS, 2, 32, 128)
    left = couplings[:, 0]
    right = couplings[:, 1]
    own_low = transfers[0]
    own_high = transfers[GROUP_BITS]
    group_table = jnp.concatenate(
        [transfers[1:GROUP_BITS], left[:GROUP_BITS][::-1]], axis=0
    )
    top_table = jnp.concatenate(
        [transfers[GROUP_BITS + 1 : TOP_BITS - 1], left[GROUP_BITS:][::-1]], axis=0
    )

    coefs, root, tables = call(
        up_kernel,
        "upward",
        [shape(LOCAL, 8, 128), shape(8, 128), shape(LOCAL, 64, 128, dtype=BF16)],
        [sources, leaf_cluster_basis, local_transfer],
    )
    coef_low = permute(coefs, forward)
    coef_high = permute(coefs, backward)

    for bit in range(TOP_BITS - 1, GROUP_BITS - 1, -1):
        low = bit - GROUP_BITS
        high = TOP_BITS - GROUP_BITS - 2 + TOP_BITS - bit
        low = min(low, TOP_BITS - GROUP_BITS - 2)
        top_table = hand_down(top_table, right[bit], device, bit, low, high)
    for bit in range(GROUP_BITS - 1, -1, -1):
        high = GROUP_BITS - 1 + GROUP_BITS - bit
        group_table = hand_down(group_table, right[bit], device, bit, bit, high)

    near = call(
        near_kernel,
        "near_field",
        shape(16, LEAVES * POINTS),
        [near_partner, near_count, index, sources, source_low, source_high, near_block],
        scalars=3,
        scratch=[pltpu.VMEM((LEAVES + 2 * REACH, 16, POINTS), F32)],
    )
    far = call(
        far_kernel,
        "far_field",
        shape(LOCAL, 8, 128),
        [
            far_partner,
            far_count,
            index,
            coefs,
            coef_low,
            coef_high,
            far_coupling.transpose(1, 0, 2),
        ],
        scalars=3,
        scratch=[pltpu.VMEM((3 * LOCAL, 8, 128), F32)],
    )

    shares = call(
        share_kernel,
        "group_shares",
        shape(GROUP, 16, 128),
        [position, root, own_low, group_table],
        scalars=1,
        scratch=[pltpu.VMEM((GROUP_BITS, 8, 128), F32)],
    )
    in_group = [list(range(first, first + GROUP)) for first in range(0, count, GROUP)]
    across = [list(range(first, count, GROUP)) for first in range(GROUP)]
    arrived = lax.all_to_all(shares, "leaf", 0, 0, axis_index_groups=in_group)
    sibling, rising = call(
        rise_kernel,
        "top_shares",
        [shape(GROUP_BITS, 8, 128), shape(GROUPS, 8, 128)],
        [position, arrived, own_high, top_table],
        scalars=1,
        scratch=[pltpu.VMEM((TOP_BITS - GROUP_BITS, 8, 128), F32)],
    )
    arrived = lax.all_to_all(rising, "leaf", 0, 0, axis_index_groups=across)
    turned = call(
        turn_kernel,
        "top_turn",
        shape(GROUP, 8, 128),
        [position, arrived, own_high, top_table],
        scalars=1,
    )
    arrived = lax.all_to_all(turned, "leaf", 0, 0, axis_index_groups=in_group)
    return call(
        down_kernel,
        "downward",
        shape(16, LEAVES * POINTS),
        [arrived, sibling, own_low, group_table, tables, far, leaf_cluster_basis, near],
        scratch=[pltpu.VMEM((LOCAL, 8, 128), F32)],
    )


def solution(mesh):
    placed = (
        P(None, "leaf"),
        P("leaf", None, None),
        P("leaf", None),
        P("leaf", None, None),
        P("leaf", None),
        P("leaf"),
        P("leaf", None, None),
        P("leaf", None, None, None),
        P("leaf", None, None, None),
        P("leaf", None),
        P("leaf"),
    )
    return jax.shard_map(
        on_device, mesh=mesh, in_specs=placed, out_specs=P(None, "leaf"), check_vma=False
    )
```

```python
import jax
import jax.numpy as jnp
from jax import lax
from jax.experimental import pallas as pl
from jax.experimental.pallas import tpu as pltpu
from jax.sharding import PartitionSpec as P

F32 = jnp.float32
BF16 = jnp.bfloat16
RANK = 64
LEAVES = 16
POINTS = 128
LOCAL = 30
SLOTS = 3
NEAR = 2
REACH = 8
GROUP_BITS = 4
TOP_BITS = 9
GROUP = 1 << GROUP_BITS
TOP_STEPS = TOP_BITS - GROUP_BITS
GROUPS = 1 << TOP_STEPS
PORTER = 1
SPLIT = 2
LAYOUT = ((16, 0), (8, 16), (4, 24), (2, 28))
VMEM_BYTES = 20 * 1024 * 1024


def split(x):
    high = x.astype(BF16)
    return high, (x - high.astype(F32)).astype(BF16)


def lanes(rows):
    return lax.broadcasted_iota(jnp.int32, (rows, 128), 1)


def table_form(table):
    high, low = split(table)
    return jnp.concatenate([high, low, high, low], axis=0)


def coef_form(packed):
    lane = lanes(8)
    even = 2 * (lane % 32)
    parts = [
        jnp.take_along_axis(packed, even + shift, axis=1) for shift in (0, 64, 1, 65)
    ]
    full = jnp.concatenate(parts, axis=0)
    high, low = split(full)
    return jnp.where(lanes(32) < 64, high.astype(F32), low.astype(F32)).astype(BF16)


def dot(a, b):
    return lax.dot_general(a, b, (((1,), (0,)), ((), ())), preferred_element_type=F32)


def dot_t(a, b):
    return lax.dot_general(a, b, (((1,), (1,)), ((), ())), preferred_element_type=F32)


def fold(out):
    left = lanes(8) < 64
    straight = jnp.where(left, out[0:8], out[24:32])
    crossed = jnp.where(left, out[8:16], out[16:24])
    return straight + pltpu.roll(crossed, 64, 1)


def times(packed, table):
    return fold(dot(coef_form(packed), table_form(table)))


def row_form(packed):
    left = lanes(8) < 64
    turned = pltpu.roll(packed, 64, 1)
    zero = jnp.zeros_like(packed)
    full = jnp.concatenate(
        [
            jnp.where(left, packed, zero),
            jnp.where(left, turned, zero),
            jnp.where(left, zero, turned),
            jnp.where(left, zero, packed),
        ],
        axis=0,
    )
    return split(full)


def weave(even_odd):
    lane = lanes(8)
    place = (lane % 64) // 2
    wide = jnp.concatenate([even_odd] * 4, axis=1)
    pick = [jnp.take_along_axis(wide[8 * k : 8 * k + 8], place, axis=1) for k in range(4)]
    even = lane % 2 == 0
    return jnp.where(
        lane < 64, jnp.where(even, pick[0], pick[2]), jnp.where(even, pick[1], pick[3])
    )


def times_t_raw(rows, high, low):
    row_high, row_low = rows
    both = dot_t(jnp.concatenate([row_high, row_low], axis=0), high)
    return both[:32] + both[32:] + dot_t(row_high, low)


def times_t(packed, table):
    high, low = split(table)
    return weave(times_t_raw(row_form(packed), high, low))


def unpack(packed):
    return jnp.concatenate([packed[:, :RANK], packed[:, RANK:]], axis=0)


def pack(value):
    return jnp.concatenate([value[:8], value[8:]], axis=1)


def place_of_device():
    device = lax.axis_index("leaf").astype(jnp.int32)
    return device, device & (GROUP - 1), device >> GROUP_BITS


def up_kernel(sources, basis, transfer, coefs, root, tables, forward, backward):
    table = transfer[...].reshape(LOCAL, 32, 128)
    for row in range(LOCAL):
        high, low = split(table[row])
        tables[row, 0:32] = high
        tables[row, 32:64] = low
    for leaf in range(LEAVES):
        entries = sources[:, leaf * POINTS : (leaf + 1) * POINTS]
        edge, place = (backward, leaf) if leaf < REACH else (forward, leaf - REACH)
        edge[LOCAL + 2 * place] = entries[:8]
        edge[LOCAL + 2 * place + 1] = entries[8:]
        high, low = split(entries)
        basis_high, basis_low = split(basis[leaf])
        both = dot_t(jnp.concatenate([high, low], axis=0), basis_high)
        coefs[leaf] = pack(both[:16] + both[16:] + dot_t(high, basis_low))
    for level, (clusters, offset) in enumerate(LAYOUT):
        for parent in range(clusters // 2):
            first = offset + 2 * parent
            left = jnp.concatenate(
                [coef_form(coefs[first]), coef_form(coefs[first + 1])], axis=1
            )
            halves = [tables[first], tables[first], tables[first + 1], tables[first + 1]]
            value = fold(dot(left, jnp.concatenate(halves, axis=0)))
            if clusters > 2:
                coefs[offset + clusters + parent] = value
            else:
                root[...] = value
    forward[0:LOCAL] = coefs[...]
    backward[0:LOCAL] = coefs[...]


def near_kernel(partner, count, own, low, high, block, out, leaves):
    for leaf in range(LEAVES):
        leaves[REACH + leaf] = own[:, leaf * POINTS : (leaf + 1) * POINTS]
    for leaf in range(REACH):
        for half in range(2):
            rows = slice(8 * half, 8 * half + 8)
            leaves[leaf, rows] = low[LOCAL + 2 * leaf + half]
            leaves[REACH + LEAVES + leaf, rows] = high[LOCAL + 2 * leaf + half]
    first = place_of_device()[0] * LEAVES - REACH
    for leaf in range(LEAVES):
        total = None
        for slot in range(NEAR):
            place = jnp.clip(partner[slot, leaf] - first, 0, LEAVES + 2 * REACH - 1)
            used = (slot < count[leaf]).astype(F32)
            picked_high, picked_low = split(leaves[place] * used)
            block_high, block_low = split(block[leaf, slot])
            both = dot_t(jnp.concatenate([picked_high, picked_low], axis=0), block_high)
            value = both[:16] + both[16:] + dot_t(picked_high, block_low)
            total = value if total is None else total + value
        out[:, leaf * POINTS : (leaf + 1) * POINTS] = total


def far_kernel(partner, count, own, low, high, coupling, out, extended):
    device = place_of_device()[0]
    extended[0:LOCAL] = low[0:LOCAL]
    extended[LOCAL : 2 * LOCAL] = own[...]
    extended[2 * LOCAL : 3 * LOCAL] = high[0:LOCAL]
    tables = [coupling[slot].reshape(LOCAL, 32, 128) for slot in range(SLOTS)]
    for clusters, offset in LAYOUT:
        for cluster in range(clusters):
            row = offset + cluster
            left = []
            right = []
            for slot in range(SLOTS):
                index = partner[slot, row]
                side = jnp.clip(index // clusters - device + 1, 0, 2)
                place = side * LOCAL + offset + index % clusters
                used = (slot < count[row]).astype(F32)
                left.append(coef_form(extended[place] * used))
                right.append(table_form(tables[slot][row]))
            out[row] = fold(dot(jnp.concatenate(left, axis=1), jnp.concatenate(right, axis=0)))


def gather_tables(transfers, couplings, group_raw, high_raw, low_raw, group_pay):
    for level in range(GROUP_BITS):
        group_raw[level] = transfers[level]
        for side in range(2):
            group_raw[GROUP_BITS * (1 + side) + level] = couplings[level, :, side, :]
    for level in range(TOP_STEPS):
        half, (transfer, *sides) = top_place(level)
        raw = (low_raw, high_raw)[half]
        if transfer is not None:
            raw[transfer] = transfers[GROUP_BITS + level]
        for side in range(2):
            raw[sides[side]] = couplings[GROUP_BITS + level, :, side, :]
    group_pay[0] = couplings[GROUP_BITS - 1, :, 1, :]


def group_place(level):
    return level, GROUP_BITS + level, 2 * GROUP_BITS + level


def top_place(level):
    if level < SPLIT:
        return 0, (level, SPLIT + level, 2 * SPLIT + level)
    place = level - SPLIT
    size = TOP_STEPS - SPLIT
    transfer = place if level < TOP_STEPS - 1 else None
    return 1, (transfer, size - 1 + place, 2 * size - 1 + place)


def group_entries(raw, level):
    _, left, right = group_place(level)
    above = raw[level + 1] if level + 1 < GROUP_BITS else None
    return above, raw[left], raw[right]


def top_entries(raws, level):
    half, (_, left, right) = top_place(level)
    above = None
    if level + 2 < TOP_STEPS:
        upper, (transfer, _, _) = top_place(level + 1)
        above = raws[upper][transfer]
    return above, raws[half][left], raws[half][right]


def write_payload(entries, live, pay):
    above, _, right = entries
    place = 0
    if above is not None:
        pay[0] = above
        place = 1
    if live is not None:
        pay[place : place + live.shape[0]] = live[...]
        place += live.shape[0]
    pay[place] = right


def merge(entries, live, arrived, out, flag):
    above, left, _ = entries
    size = out.shape[0]
    right_child = flag == 1
    start = 0
    if above is not None:
        out[0] = jnp.where(right_child, arrived[0], above)
        start = 1
    for entry in range(start, size - 1):
        out[entry] = jnp.where(right_child, arrived[entry], live[entry - start])
    out[size - 1] = jnp.where(right_child, arrived[size - 1], left)


def call(kernel, name, outs, args, scalars=0, scratch=(), after=(), flops=0):
    vmem = pl.BlockSpec(memory_space=pltpu.VMEM)
    smem = pl.BlockSpec(memory_space=pltpu.SMEM)
    spare = pl.BlockSpec(memory_space=pl.ANY)
    given = len(args)

    def body(*refs):
        kernel(*refs[:given], *refs[given + len(after) :])

    single = not isinstance(outs, list)
    return pl.pallas_call(
        body,
        out_shape=outs,
        in_specs=[smem] * scalars + [vmem] * (given - scalars) + [spare] * len(after),
        out_specs=vmem if single else [vmem] * len(outs),
        scratch_shapes=list(scratch),
        compiler_params=pltpu.CompilerParams(vmem_limit_bytes=VMEM_BYTES),
        cost_estimate=pl.CostEstimate(
            flops=flops, bytes_accessed=flops // 400, transcendentals=0
        ),
        name=name,
    )(*args, *after)


def shape(*dims, dtype=F32):
    return jax.ShapeDtypeStruct(dims, dtype)


def permute(value, pairs):
    return lax.ppermute(value, "leaf", pairs)


def step_pairs(count, bit, member=0):
    return [(i + member, i + member + (1 << bit)) for i in range(0, count, 2 << bit)]


def group_size(bit):
    return 2 * (GROUP_BITS - bit) - 1


def top_size(bit):
    left = TOP_BITS - bit
    return left + max(left - 2, 0)


def share_kernel(root, raw, live, arrived, blocks, table, chain):
    _, member, _ = place_of_device()
    merge(group_entries(raw, 0), live, arrived, table, member & 1)
    value = root[...]
    chain[0] = value
    for level in range(GROUP_BITS):
        value = times(value, raw[0] if level == 0 else table[level - 1])
        if level + 1 < GROUP_BITS:
            chain[level + 1] = value
    for other in range(GROUP):
        apart = member ^ other
        level = sum((apart >= (1 << bit)).astype(jnp.int32) for bit in range(1, GROUP_BITS))
        blocks[other, 0:8] = chain[level]
        blocks[other, 8:16] = value


def rise_kernel(given, low_raw, high_raw, live, arrived, sibling, blocks, table, chain):
    _, member, group = place_of_device()
    merge(top_entries((low_raw, high_raw), 0), live, arrived, table, group & 1)
    for level in range(GROUP_BITS):
        total = None
        for apart in range(1 << level, 2 << level):
            value = given[member ^ apart, 0:8]
            total = value if total is None else total + value
        sibling[level] = total
    value = given[0, 8:16]
    for other in range(1, GROUP):
        value = value + given[other, 8:16]
    chain[0] = value
    for level in range(TOP_STEPS - 1):
        value = times(value, low_raw[0] if level == 0 else table[level - 1])
        chain[level + 1] = value
    for other in range(GROUPS):
        apart = group ^ other
        level = sum((apart >= (1 << bit)).astype(jnp.int32) for bit in range(1, TOP_STEPS))
        blocks[other] = chain[level]


def turn_kernel(given, raw, table, out):
    _, _, group = place_of_device()
    terms = []
    for level in range(TOP_STEPS):
        total = None
        for apart in range(1 << level, 2 << level):
            piece = given[group ^ apart]
            total = piece if total is None else total + piece
        terms.append(times(total, table[2 * TOP_STEPS - 3 - level]))
    value = terms[TOP_STEPS - 1]
    for level in range(TOP_STEPS - 2, -1, -1):
        value = times_t(value, raw[0] if level == 0 else table[level - 1]) + terms[level]
    for other in range(GROUP):
        out[other] = value


def down_kernel(given, sibling, raw, table, tables, far, basis, near, out):
    value = given[PORTER]
    terms = [
        times(sibling[level], table[2 * GROUP_BITS - 2 - level]) for level in range(GROUP_BITS)
    ]
    for level in range(GROUP_BITS - 1, -1, -1):
        value = times_t(value, raw[0] if level == 0 else table[level - 1]) + terms[level]
    parents = [value]
    for clusters, offset in reversed(LAYOUT):
        following = []
        for parent in range(clusters // 2):
            first = offset + 2 * parent
            high = jnp.concatenate([tables[first, 0:32], tables[first + 1, 0:32]], axis=0)
            low = jnp.concatenate([tables[first, 32:64], tables[first + 1, 32:64]], axis=0)
            out_pair = times_t_raw(row_form(parents[parent]), high, low)
            following.append(weave(out_pair[:, 0:32]) + far[first])
            following.append(weave(out_pair[:, 32:64]) + far[first + 1])
        parents = following
    for leaf in range(LEAVES):
        high, low = split(unpack(parents[leaf]))
        basis_high, basis_low = split(basis[leaf])
        both = dot(jnp.concatenate([high, low], axis=0), basis_high)
        place = slice(leaf * POINTS, (leaf + 1) * POINTS)
        out[:, place] = both[:16] + both[16:] + dot(high, basis_low) + near[:, place]


def on_device(
    sources,
    leaf_cluster_basis,
    local_transfer,
    far_coupling,
    far_partner,
    far_count,
    top_transfer,
    top_coupling,
    near_block,
    near_partner,
    near_count,
):
    count = lax.axis_size("leaf")
    forward = [(i, i + 1) for i in range(count - 1)]
    backward = [(i + 1, i) for i in range(count - 1)]

    transfers = top_transfer.reshape(TOP_BITS, 32, 128)
    couplings = top_coupling.reshape(TOP_BITS, 2, 32, 128).transpose(0, 2, 1, 3)
    size = TOP_STEPS - SPLIT
    group_raw, high_raw, low_raw, group_pay = call(
        gather_tables,
        "top_tables",
        [
            shape(3 * GROUP_BITS, 32, 128),
            shape(3 * size - 1, 32, 128),
            shape(3 * SPLIT, 32, 128),
            shape(1, 32, 128),
        ],
        [transfers, couplings],
        flops=1 << 30,
    )
    to_porter = [(i, i + PORTER) for i in range(0, count, GROUP)]
    high_raw = permute(high_raw, to_porter)
    group_in = permute(group_pay, step_pairs(count, GROUP_BITS - 1))
    low_raw = permute(low_raw, to_porter)

    coefs, root, tables, low_edge, high_edge = call(
        up_kernel,
        "upward",
        [
            shape(LOCAL, 8, 128),
            shape(8, 128),
            shape(LOCAL, 64, 128, dtype=BF16),
            shape(LOCAL + 2 * REACH, 8, 128),
            shape(LOCAL + 2 * REACH, 8, 128),
        ],
        [sources, leaf_cluster_basis, local_transfer],
        flops=2 << 30,
    )
    low = permute(low_edge, forward)
    high = permute(high_edge, backward)

    group_live = None
    top_live = None
    top_in = None
    for step in range(GROUP_BITS - 1):
        bit = GROUP_BITS - 1 - step
        top_bit = TOP_BITS - step

        def joint(*refs, bit=bit, top_bit=top_bit, step=step):
            refs = list(refs)
            raw, arrived = refs.pop(0), refs.pop(0)
            live = refs.pop(0) if step else None
            raws = (None, refs.pop(0))
            upper_arrived = refs.pop(0) if step else None
            upper_live = refs.pop(0) if step > 1 else None
            out, pay = refs.pop(0), refs.pop(0)
            _, member, group = place_of_device()
            merge(group_entries(raw, bit), live, arrived, out, (member >> bit) & 1)
            write_payload(group_entries(raw, bit - 1), out, pay)
            upper_out = None
            level = top_bit - GROUP_BITS
            if step:
                upper_out = refs.pop(0)
                entries = top_entries(raws, level)
                merge(entries, upper_live, upper_arrived, upper_out, (group >> level) & 1)
            write_payload(top_entries(raws, level - 1), upper_out, refs.pop(0))

        args = [group_raw, group_in]
        if step:
            args.append(group_live)
        args.append(high_raw)
        if step:
            args.append(top_in)
        if step > 1:
            args.append(top_live)
        outs = [shape(group_size(bit), 32, 128), shape(group_size(bit - 1), 32, 128)]
        if step:
            outs.append(shape(top_size(top_bit), 32, 128))
        outs.append(shape(top_size(top_bit - 1), 32, 128))
        results = list(call(joint, f"hand_down_{step}", outs, args, flops=1 << 29))
        group_live, group_pay = results[0], results[1]
        if step:
            top_live = results[2]
        top_pay = results[-1]
        group_in = permute(group_pay, step_pairs(count, bit - 1))
        top_in = permute(top_pay, step_pairs(count, top_bit - 1, PORTER))

    def step_up(bit, live, arrived, after=()):
        def lone(low, high, live, arrived, out, pay):
            level = bit - GROUP_BITS
            _, _, group = place_of_device()
            merge(top_entries((low, high), level), live, arrived, out, (group >> level) & 1)
            write_payload(top_entries((low, high), level - 1), out, pay)

        return call(
            lone,
            f"hand_down_top_{bit}",
            [shape(top_size(bit), 32, 128), shape(top_size(bit - 1), 32, 128)],
            [low_raw, high_raw, live, arrived],
            flops=1 << 29,
            after=after,
        )

    bit = TOP_BITS - GROUP_BITS + 1
    top_live, top_pay = step_up(bit, top_live, top_in)
    shares, group_table = call(
        share_kernel,
        "group_shares",
        [shape(GROUP, 16, 128), shape(2 * GROUP_BITS - 1, 32, 128)],
        [root, group_raw, group_live, group_in],
        scratch=[pltpu.VMEM((GROUP_BITS, 8, 128), F32)],
        after=[top_live],
        flops=2 << 30,
    )
    in_group = [list(range(first, first + GROUP)) for first in range(0, count, GROUP)]
    across = [list(range(first, count, GROUP)) for first in range(GROUP)]
    group_given = lax.all_to_all(shares, "leaf", 0, 0, axis_index_groups=in_group)
    top_in = permute(top_pay, step_pairs(count, bit - 1, PORTER))
    for bit in range(bit - 1, GROUP_BITS, -1):
        top_live, top_pay = step_up(bit, top_live, top_in)
        top_in = permute(top_pay, step_pairs(count, bit - 1, PORTER))

    sibling, rising, top_table = call(
        rise_kernel,
        "top_shares",
        [shape(GROUP_BITS, 8, 128), shape(GROUPS, 8, 128), shape(2 * TOP_STEPS - 2, 32, 128)],
        [group_given, low_raw, high_raw, top_live, top_in],
        scratch=[pltpu.VMEM((TOP_STEPS, 8, 128), F32)],
        flops=2 << 30,
    )
    top_given = lax.all_to_all(rising, "leaf", 0, 0, axis_index_groups=across)

    near = call(
        near_kernel,
        "near_field",
        shape(16, LEAVES * POINTS),
        [near_partner.T, near_count, sources, low, high, near_block],
        scalars=2,
        scratch=[pltpu.VMEM((LEAVES + 2 * REACH, 16, POINTS), F32)],
        flops=2 << 30,
    )
    far = call(
        far_kernel,
        "far_field",
        shape(LOCAL, 8, 128),
        [far_partner.T, far_count, coefs, low, high, far_coupling.transpose(1, 0, 2)],
        scalars=2,
        scratch=[pltpu.VMEM((3 * LOCAL, 8, 128), F32)],
        flops=2 << 30,
    )
    turned = call(
        turn_kernel,
        "top_turn",
        shape(GROUP, 8, 128),
        [top_given, low_raw, top_table],
        after=[near, far],
        flops=2 << 30,
    )
    given = lax.all_to_all(turned, "leaf", 0, 0, axis_index_groups=in_group)
    return call(
        down_kernel,
        "downward",
        shape(16, LEAVES * POINTS),
        [given, sibling, group_raw, group_table, tables, far, leaf_cluster_basis, near],
        flops=4 << 30,
    )


def solution(mesh):
    placed = (
        P(None, "leaf"),
        P("leaf", None, None),
        P("leaf", None),
        P("leaf", None, None),
        P("leaf", None),
        P("leaf"),
        P("leaf", None, None),
        P("leaf", None, None, None),
        P("leaf", None, None, None),
        P("leaf", None),
        P("leaf"),
    )
    return jax.shard_map(
        on_device, mesh=mesh, in_specs=placed, out_specs=P(None, "leaf"), check_vma=False
    )
```

```python
import jax
import jax.numpy as jnp
from jax import lax
from jax.experimental import pallas as pl
from jax.experimental.pallas import tpu as pltpu
from jax.sharding import PartitionSpec as P

F32 = jnp.float32
BF16 = jnp.bfloat16
RANK = 64
LEAVES = 16
POINTS = 128
LOCAL = 30
SLOTS = 3
NEAR = 2
REACH = 8
GROUP_BITS = 4
TOP_BITS = 9
GROUP = 1 << GROUP_BITS
PORTER = 1
LAYOUT = ((16, 0), (8, 16), (4, 24), (2, 28))
VMEM_BYTES = 20 * 1024 * 1024
WIDE_BYTES = 63 * 1024 * 1024


def split(x):
    high = x.astype(BF16)
    return high, (x - high.astype(F32)).astype(BF16)


def lanes(rows):
    return lax.broadcasted_iota(jnp.int32, (rows, 128), 1)


def table_form(table):
    high, low = split(table)
    return jnp.concatenate([high, low, high, low], axis=0)


def coef_form(packed):
    lane = lanes(packed.shape[0])
    even = 2 * (lane % 32)
    parts = [
        jnp.take_along_axis(packed, even + shift, axis=1) for shift in (0, 64, 1, 65)
    ]
    full = jnp.concatenate(parts, axis=0)
    high, low = split(full)
    return jnp.where(lanes(full.shape[0]) < 64, high.astype(F32), low.astype(F32)).astype(BF16)


def dot(a, b):
    return lax.dot_general(a, b, (((1,), (0,)), ((), ())), preferred_element_type=F32)


def dot_t(a, b):
    return lax.dot_general(a, b, (((1,), (1,)), ((), ())), preferred_element_type=F32)


def fold(out):
    rows = out.shape[0] // 4
    left = lanes(rows) < 64
    straight = jnp.where(left, out[0:rows], out[3 * rows :])
    crossed = jnp.where(left, out[rows : 2 * rows], out[2 * rows : 3 * rows])
    return straight + pltpu.roll(crossed, 64, 1)


def times(packed, table):
    return fold(dot(coef_form(packed), table_form(table)))


def row_form(packed):
    left = lanes(8) < 64
    turned = pltpu.roll(packed, 64, 1)
    zero = jnp.zeros_like(packed)
    full = jnp.concatenate(
        [
            jnp.where(left, packed, zero),
            jnp.where(left, turned, zero),
            jnp.where(left, zero, turned),
            jnp.where(left, zero, packed),
        ],
        axis=0,
    )
    return split(full)


def weave(even_odd):
    lane = lanes(8)
    place = (lane % 64) // 2
    wide = jnp.concatenate([even_odd] * 4, axis=1)
    pick = [jnp.take_along_axis(wide[8 * k : 8 * k + 8], place, axis=1) for k in range(4)]
    even = lane % 2 == 0
    return jnp.where(
        lane < 64, jnp.where(even, pick[0], pick[2]), jnp.where(even, pick[1], pick[3])
    )


def times_t_raw(rows, high, low):
    row_high, row_low = rows
    both = dot_t(jnp.concatenate([row_high, row_low], axis=0), high)
    return both[:32] + both[32:] + dot_t(row_high, low)


def times_t(packed, table):
    high, low = split(table)
    return weave(times_t_raw(row_form(packed), high, low))


def unpack(packed):
    return jnp.concatenate([packed[:, :RANK], packed[:, RANK:]], axis=0)


def pack(value):
    return jnp.concatenate([value[:8], value[8:]], axis=1)


def place_of_device():
    device = lax.axis_index("leaf").astype(jnp.int32)
    return device, device & (GROUP - 1), device >> GROUP_BITS


def up_kernel(sources, basis, transfer, coefs, root, tables):
    table = transfer[...].reshape(LOCAL, 32, 128)
    for row in range(LOCAL):
        high, low = split(table[row])
        tables[row, 0:32] = high
        tables[row, 32:64] = low
    for leaf in range(LEAVES):
        entries = sources[:, leaf * POINTS : (leaf + 1) * POINTS]
        high, low = split(entries)
        basis_high, basis_low = split(basis[leaf])
        both = dot_t(jnp.concatenate([high, low], axis=0), basis_high)
        coefs[leaf] = pack(both[:16] + both[16:] + dot_t(high, basis_low))
    for level, (clusters, offset) in enumerate(LAYOUT):
        for parent in range(clusters // 2):
            first = offset + 2 * parent
            left = jnp.concatenate(
                [coef_form(coefs[first]), coef_form(coefs[first + 1])], axis=1
            )
            halves = [tables[first], tables[first], tables[first + 1], tables[first + 1]]
            value = fold(dot(left, jnp.concatenate(halves, axis=0)))
            if clusters > 2:
                coefs[offset + clusters + parent] = value
            else:
                root[...] = value


def edge_kernel(sources, coefs, forward, backward):
    forward[0:LOCAL] = coefs[...]
    backward[0:LOCAL] = coefs[...]
    for leaf in range(LEAVES):
        edge, place = (backward, leaf) if leaf < REACH else (forward, leaf - REACH)
        entries = sources[:, leaf * POINTS : (leaf + 1) * POINTS]
        edge[LOCAL + 2 * place] = entries[:8]
        edge[LOCAL + 2 * place + 1] = entries[8:]


def near_kernel(partner, count, own, low, high, block, out, leaves):
    for leaf in range(LEAVES):
        leaves[REACH + leaf] = own[:, leaf * POINTS : (leaf + 1) * POINTS]
    for leaf in range(REACH):
        for half in range(2):
            rows = slice(8 * half, 8 * half + 8)
            leaves[leaf, rows] = low[LOCAL + 2 * leaf + half]
            leaves[REACH + LEAVES + leaf, rows] = high[LOCAL + 2 * leaf + half]
    first = place_of_device()[0] * LEAVES - REACH
    for leaf in range(LEAVES):
        total = None
        for slot in range(NEAR):
            place = jnp.clip(partner[slot, leaf] - first, 0, LEAVES + 2 * REACH - 1)
            used = (slot < count[leaf]).astype(F32)
            picked_high, picked_low = split(leaves[place] * used)
            block_high, block_low = split(block[leaf, slot])
            both = dot_t(jnp.concatenate([picked_high, picked_low], axis=0), block_high)
            value = both[:16] + both[16:] + dot_t(picked_high, block_low)
            total = value if total is None else total + value
        out[:, leaf * POINTS : (leaf + 1) * POINTS] = total


def far_kernel(partner, count, own, low, high, coupling, out, extended):
    device = place_of_device()[0]
    extended[0:LOCAL] = low[0:LOCAL]
    extended[LOCAL : 2 * LOCAL] = own[...]
    extended[2 * LOCAL : 3 * LOCAL] = high[0:LOCAL]
    tables = [coupling[slot].reshape(LOCAL, 32, 128) for slot in range(SLOTS)]
    for clusters, offset in LAYOUT:
        for cluster in range(clusters):
            row = offset + cluster
            left = []
            right = []
            for slot in range(SLOTS):
                index = partner[slot, row]
                side = jnp.clip(index // clusters - device + 1, 0, 2)
                place = side * LOCAL + offset + index % clusters
                used = (slot < count[row]).astype(F32)
                left.append(coef_form(extended[place] * used))
                right.append(table_form(tables[slot][row]))
            out[row] = fold(dot(jnp.concatenate(left, axis=1), jnp.concatenate(right, axis=0)))


def call(kernel, name, outs, args, lazy=(), scalars=0, scratch=(), after=(), flops=0):
    vmem = pl.BlockSpec(memory_space=pltpu.VMEM)
    smem = pl.BlockSpec(memory_space=pltpu.SMEM)
    spare = pl.BlockSpec(memory_space=pl.ANY)
    given, slow, spares = len(args), len(lazy), len(after)

    def body(*refs):
        own = refs[given + slow + spares :]
        copies = []
        getters = []
        if slow:
            own, targets, semaphores = own[: -slow - 1], own[-slow - 1 : -1], own[-1]
            for i, target in enumerate(targets):
                copies.append(
                    pltpu.make_async_copy(refs[given + i], target, semaphores.at[i])
                )
                copies[-1].start()
            waiting = set(range(slow))

            def getter(i):
                def get():
                    if i in waiting:
                        waiting.remove(i)
                        copies[i].wait()
                    return targets[i]

                return get

            getters = [getter(i) for i in range(slow)]
        kernel(*refs[:given], *getters, *own)
        for get in getters:
            get()

    buffers = [pltpu.VMEM(item.shape, item.dtype) for item in lazy]
    if lazy:
        buffers.append(pltpu.SemaphoreType.DMA((slow,)))
    result = pl.pallas_call(
        body,
        out_shape=list(outs),
        in_specs=[smem] * scalars + [vmem] * (given - scalars) + [spare] * (slow + spares),
        out_specs=[vmem] * len(outs),
        scratch_shapes=list(scratch) + buffers,
        compiler_params=pltpu.CompilerParams(
            vmem_limit_bytes=WIDE_BYTES if lazy else VMEM_BYTES
        ),
        cost_estimate=pl.CostEstimate(
            flops=flops, bytes_accessed=flops // 400, transcendentals=0
        ),
        name=name,
    )(*args, *lazy, *after)
    return result if len(result) > 1 else result[0]


def shape(*dims, dtype=F32):
    return jax.ShapeDtypeStruct(dims, dtype)


def permute(value, pairs):
    return lax.ppermute(value, "leaf", pairs)


def tables(size):
    return shape(size, 32, 128)


def prepare_kernel(transfers, couplings, group_raw, high_raw, low_raw, group_pay):

    def coupling(level, side):
        return couplings[level - 1, :, side, :]

    group_pay[0] = coupling(GROUP_BITS, 1)
    high_raw[0] = transfers[7]
    low_raw[0:3] = transfers[4:7]
    for side in range(2):
        for level in range(7, 10):
            high_raw[1 + 3 * side + level - 7] = coupling(level, side)
        for level in range(5, 7):
            low_raw[3 + 2 * side + level - 5] = coupling(level, side)
        for level in range(1, 5):
            group_raw[4 + 4 * side + level - 1] = coupling(level, side)
    group_raw[0:4] = transfers[0:4]


def choose(flag, first, second):
    return jnp.where(flag, first, second)


def merge_group(raw, bit, live, arrived, out):
    _, member, _ = place_of_device()
    right_child = ((member >> bit) & 1) == 1
    size = out.shape[0]
    start = 0
    if bit + 1 < GROUP_BITS:
        out[0] = choose(right_child, arrived[0], raw[bit + 1])
        start = 1
    for entry in range(start, size - 1):
        out[entry] = choose(right_child, arrived[entry], live[entry - start])
    out[size - 1] = choose(right_child, arrived[size - 1], raw[GROUP_BITS + bit])


def group_payload(raw, bit, live, pay):
    pay[0] = raw[bit + 1]
    size = live.shape[0]
    pay[1 : 1 + size] = live[...]
    pay[1 + size] = raw[2 * GROUP_BITS + bit]


def first_kernel(raw, arrived, high_raw, live, pay, high_pay):
    merge_group(raw, 3, None, arrived, live)
    group_payload(raw, 2, live, pay)
    high_pay[0] = high_raw[6]


def second_kernel(
    raw, arrived, live, low_raw, high_raw, high_in, out, pay, high_live, high_pay, low_pay
):
    merge_group(raw, 2, live, arrived, out)
    group_payload(raw, 1, out, pay)
    _, _, group = place_of_device()
    value = choose(((group >> 4) & 1) == 1, high_in[0], high_raw[3])
    high_live[0] = value
    high_pay[0] = value
    high_pay[1] = high_raw[5]
    low_pay[0] = low_raw[2]
    low_pay[1] = low_raw[6]


def line_kernel(high_raw, high_in, high_live, upper, high_pay):
    _, _, group = place_of_device()
    right_child = ((group >> 3) & 1) == 1
    ninth = choose(right_child, high_in[0], high_live[0])
    eighth = choose(right_child, high_in[1], high_raw[2])
    for target, side in ((upper, 1), (high_pay, 4)):
        target[0] = high_raw[0]
        target[1] = ninth
        target[2] = eighth
        target[3] = high_raw[side]


def third_kernel(raw, arrived, live, low_raw, low_in, out, pay, keep, low_pay):
    merge_group(raw, 1, live, arrived, out)
    group_payload(raw, 0, out, pay)
    _, _, group = place_of_device()
    second = ((group >> 1) & 1) == 1
    sixth = choose(second, low_in[0], low_raw[2])
    sixth_coupling = choose(second, low_in[1], low_raw[4])
    for target, side in ((keep, 3), (low_pay, 5)):
        target[0] = sixth
        target[1] = sixth_coupling
        target[2] = low_raw[1]
        target[3] = low_raw[side]
    keep[4] = low_raw[0]


def fourth_kernel(upper, near_in, far_in, out):
    _, _, group = place_of_device()
    place = group & 7
    for entry in range(4):
        out[entry] = choose(
            place == 2, near_in[entry], choose(place == 6, far_in[entry], upper[entry])
        )


def share_kernel(root, raw, live, arrived, blocks, table, chain):
    _, member, _ = place_of_device()
    merge_group(raw, 0, live, arrived, table)
    value = root[...]
    chain[0] = value
    for level in range(GROUP_BITS):
        value = times(value, raw[0] if level == 0 else table[level - 1])
        if level + 1 < GROUP_BITS:
            chain[level + 1] = value
    for other in range(GROUP):
        apart = member ^ other
        level = sum((apart >= (1 << bit)).astype(jnp.int32) for bit in range(1, GROUP_BITS))
        blocks[other, 0:8] = chain[level]
        blocks[other, 8:16] = value


def total_of(pieces):
    total = pieces[0]
    for piece in pieces[1:]:
        total = total + piece
    return total


def rise_kernel(given, keep, near_in, blocks, sibling, table, chain):
    _, member, group = place_of_device()
    place = group & 7
    odd = (place & 1) == 1
    for entry in range(4):
        table[entry] = choose(odd, near_in[entry], keep[entry])
    table[4] = keep[4]
    for level in range(GROUP_BITS):
        sibling[level] = total_of(
            [given[member ^ apart, 0:8] for apart in range(1 << level, 2 << level)]
        )
    value = total_of([given[other, 8:16] for other in range(GROUP)])
    chain[0] = value
    for level in range(3):
        value = times(value, table[4 - 2 * level])
        chain[level + 1] = value
    for other in range(8):
        apart = place ^ other
        level = sum((apart >= (1 << bit)).astype(jnp.int32) for bit in range(1, 3))
        blocks[other, 0:8] = chain[level]
        blocks[other, 8:16] = value


def fifth_kernel(upper, near_in, far_in, out):
    _, _, group = place_of_device()
    place = group & 7
    for entry in range(4):
        out[entry] = choose(
            (place & 1) == 1, near_in[entry], choose(place == 4, far_in[entry], upper[entry])
        )


def middle_kernel(given, upper, arrived, blocks, upper_out, sums):
    _, _, group = place_of_device()
    place, line = group & 7, group >> 3
    for level in range(3):
        sums[level] = total_of(
            [given[place ^ apart, 0:8] for apart in range(1 << level, 2 << level)]
        )
    value = total_of([given[other, 8:16] for other in range(8)])
    table = upper_out
    for entry in range(4):
        table[entry] = choose(place == 5, arrived[entry], upper[entry])
    raised = times(value, table[0])
    for other in range(4):
        blocks[other] = choose((line ^ other) >= 2, raised, value)


def top_sums_kernel(low, upper, sums, out):
    value = times(sums[2], upper[3])
    value = times_t(value, low[2]) + times(sums[1], low[1])
    out[0:8] = times_t(value, low[4]) + times(sums[0], low[3])
    out[8:40] = times(times(low[4], low[2]), low[0])
    for entry in range(3):
        out[40 + 32 * entry : 72 + 32 * entry] = upper[entry]


def turn_kernel(given, prepared, out):
    _, _, group = place_of_device()
    line = group >> 3
    seventh = times(given[line ^ 1], prepared[104:136])
    eighth = times(given[line ^ 2] + given[line ^ 3], prepared[72:104])
    value = times_t(eighth, prepared[40:72]) + seventh
    value = times_t(value, prepared[8:40]) + prepared[0:8]
    for other in range(GROUP):
        out[other] = value


def group_sums_kernel(sibling, raw, table, out):
    terms = [
        times(sibling[level], table[2 * GROUP_BITS - 2 - level]) for level in range(GROUP_BITS)
    ]
    value = terms[GROUP_BITS - 1]
    product = raw[0]
    for level in range(GROUP_BITS - 2, -1, -1):
        value = times_t(value, raw[0] if level == 0 else table[level - 1]) + terms[level]
    for level in range(1, GROUP_BITS):
        product = times(product, table[level - 1])
    out[0:8] = value
    out[8:40] = product


def down_kernel(given, prepared, forms, far, basis, near, out):
    prepared = prepared()
    value = times_t(given[PORTER], prepared[8:40]) + prepared[0:8]
    parents = [value]
    forms, far = forms(), far()
    for clusters, offset in reversed(LAYOUT):
        following = []
        for parent in range(clusters // 2):
            first = offset + 2 * parent
            high = jnp.concatenate([forms[first, 0:32], forms[first + 1, 0:32]], axis=0)
            low = jnp.concatenate([forms[first, 32:64], forms[first + 1, 32:64]], axis=0)
            out_pair = times_t_raw(row_form(parents[parent]), high, low)
            following.append(weave(out_pair[:, 0:32]) + far[first])
            following.append(weave(out_pair[:, 32:64]) + far[first + 1])
        parents = following
    basis, near = basis(), near()
    for leaf in range(LEAVES):
        high, low = split(unpack(parents[leaf]))
        basis_high, basis_low = split(basis[leaf])
        both = dot(jnp.concatenate([high, low], axis=0), basis_high)
        place = slice(leaf * POINTS, (leaf + 1) * POINTS)
        out[:, place] = both[:16] + both[16:] + dot(high, basis_low) + near[:, place]


def on_device(
    sources,
    leaf_cluster_basis,
    local_transfer,
    far_coupling,
    far_partner,
    far_count,
    top_transfer,
    top_coupling,
    near_block,
    near_partner,
    near_count,
):
    count = lax.axis_size("leaf")
    forward = [(i, i + 1) for i in range(count - 1)]
    backward = [(i + 1, i) for i in range(count - 1)]

    def handed(value, period, first, second):
        return permute(value, [(i + first, i + second) for i in range(0, count, period)])

    transfers = top_transfer.reshape(TOP_BITS, 32, 128)
    couplings = top_coupling.reshape(TOP_BITS, 2, 32, 128).transpose(0, 2, 1, 3)
    raw, high_raw, low_raw, pay = call(
        prepare_kernel,
        "top_tables",
        [tables(12), tables(7), tables(7), tables(1)],
        [transfers, couplings],
        flops=1 << 30,
    )
    high_raw = handed(high_raw, GROUP, 0, PORTER)
    group_in = handed(pay, 16, 0, 8)
    low_raw = handed(low_raw, GROUP, 0, PORTER)

    coefs, root, forms = call(
        up_kernel,
        "upward",
        [
            shape(LOCAL, 8, 128),
            shape(8, 128),
            shape(LOCAL, 64, 128, dtype=BF16),
        ],
        [sources, leaf_cluster_basis, local_transfer],
        flops=2 << 30,
    )
    live, pay, high_pay = call(
        first_kernel,
        "hand_down_1",
        [tables(1), tables(3), tables(1)],
        [raw, group_in, high_raw],
        flops=1 << 29,
    )
    group_in = handed(pay, 8, 0, 4)
    high_in = handed(high_pay, 512, PORTER, 256 + PORTER)
    live, pay, high_live, high_pay, low_pay = call(
        second_kernel,
        "hand_down_2",
        [tables(3), tables(5), tables(1), tables(2), tables(2)],
        [raw, group_in, live, low_raw, high_raw, high_in],
        after=[root],
        flops=1 << 29,
    )
    group_in = handed(pay, 4, 0, 2)
    high_in = handed(high_pay, 256, PORTER, 128 + PORTER)
    low_in = handed(low_pay, 64, PORTER, 32 + PORTER)
    upper, high_pay = call(
        line_kernel,
        "hand_down_line",
        [tables(4), tables(4)],
        [high_raw, high_in, high_live],
        flops=1 << 29,
    )
    near_in = handed(upper, 128, PORTER, 32 + PORTER)
    far_in = handed(high_pay, 128, PORTER, 96 + PORTER)
    upper = call(
        fourth_kernel, "hand_down_4", [tables(4)], [upper, near_in, far_in], flops=1 << 29
    )
    live, pay, keep, low_pay = call(
        third_kernel,
        "hand_down_3",
        [tables(5), tables(7), tables(5), tables(4)],
        [raw, group_in, live, low_raw, low_in],
        after=[upper],
        flops=1 << 29,
    )
    group_in = handed(pay, 2, 0, 1)
    low_in = handed(low_pay, 32, PORTER, 16 + PORTER)
    near_in = handed(upper, 32, PORTER, 16 + PORTER)
    far_in = handed(upper, 128, 96 + PORTER, 64 + PORTER)
    upper = call(
        fifth_kernel,
        "hand_down_5",
        [tables(4)],
        [upper, near_in, far_in],
        flops=1 << 29,
    )
    shares, group_table = call(
        share_kernel,
        "group_shares",
        [shape(GROUP, 16, 128), tables(7)],
        [root, raw, live, group_in],
        scratch=[pltpu.VMEM((GROUP_BITS, 8, 128), F32)],
        after=[upper],
        flops=2 << 30,
    )
    in_group = [list(range(first, first + GROUP)) for first in range(0, count, GROUP)]
    in_column = [
        list(range(line + member, line + 128, GROUP))
        for line in range(0, count, 128)
        for member in range(GROUP)
    ]
    in_line = [list(range(first, count, 128)) for first in range(128)]
    given = lax.all_to_all(shares, "leaf", 0, 0, axis_index_groups=in_group)
    blocks, sibling, low_table = call(
        rise_kernel,
        "column_shares",
        [shape(8, 16, 128), shape(GROUP_BITS, 8, 128), tables(5)],
        [given, keep, low_in],
        scratch=[pltpu.VMEM((4, 8, 128), F32)],
        flops=2 << 30,
    )
    given = lax.all_to_all(blocks, "leaf", 0, 0, axis_index_groups=in_column)
    low_edge, high_edge = call(
        edge_kernel,
        "edges",
        [shape(LOCAL + 2 * REACH, 8, 128)] * 2,
        [sources, coefs],
        after=[blocks],
        flops=1 << 29,
    )
    low_edge = permute(low_edge, forward)
    high_edge = permute(high_edge, backward)
    upper_in = handed(upper, 128, 64 + PORTER, 80 + PORTER)
    blocks, upper, sums = call(
        middle_kernel,
        "line_shares",
        [shape(4, 8, 128), tables(4), shape(3, 8, 128)],
        [given, upper, upper_in],
        flops=1 << 30,
    )
    given = lax.all_to_all(blocks, "leaf", 0, 0, axis_index_groups=in_line)

    near = call(
        near_kernel,
        "near_field",
        [shape(16, LEAVES * POINTS)],
        [near_partner.T, near_count, sources, low_edge, high_edge, near_block],
        scalars=2,
        scratch=[pltpu.VMEM((LEAVES + 2 * REACH, 16, POINTS), F32)],
        flops=2 << 30,
    )
    far = call(
        far_kernel,
        "far_field",
        [shape(LOCAL, 8, 128)],
        [far_partner.T, far_count, coefs, low_edge, high_edge, far_coupling.transpose(1, 0, 2)],
        scalars=2,
        scratch=[pltpu.VMEM((3 * LOCAL, 8, 128), F32)],
        after=[blocks],
        flops=2 << 30,
    )
    prepared = call(
        top_sums_kernel,
        "top_sums",
        [shape(136, 128)],
        [low_table, upper, sums],
        flops=1 << 30,
    )
    turned = call(
        turn_kernel,
        "top_turn",
        [shape(GROUP, 8, 128)],
        [given, prepared],
        after=[far],
        flops=2 << 30,
    )
    prepared = call(
        group_sums_kernel,
        "group_sums",
        [shape(40, 128)],
        [sibling, raw, group_table],
        flops=1 << 30,
    )
    given = lax.all_to_all(turned, "leaf", 0, 0, axis_index_groups=in_group)
    return call(
        down_kernel,
        "downward",
        [shape(16, LEAVES * POINTS)],
        [given],
        lazy=[prepared, forms, far, leaf_cluster_basis, near],
        flops=4 << 30,
    )


def solution(mesh):
    placed = (
        P(None, "leaf"),
        P("leaf", None, None),
        P("leaf", None),
        P("leaf", None, None),
        P("leaf", None),
        P("leaf"),
        P("leaf", None, None),
        P("leaf", None, None, None),
        P("leaf", None, None, None),
        P("leaf", None),
        P("leaf"),
    )
    return jax.shard_map(
        on_device, mesh=mesh, in_specs=placed, out_specs=P(None, "leaf"), check_vma=False
    )
```

```python
import jax
import jax.numpy as jnp
from jax import lax
from jax.experimental import pallas as pl
from jax.experimental.pallas import tpu as pltpu
from jax.sharding import PartitionSpec as P

F32 = jnp.float32
BF16 = jnp.bfloat16
RANK = 64
LEAVES = 16
POINTS = 128
LOCAL = 30
SLOTS = 3
NEAR = 2
REACH = 8
GROUP_BITS = 4
TOP_BITS = 9
GROUP = 1 << GROUP_BITS
NEAR_ROWS = 16 * LEAVES
PORTER = 1
HIGH = 7
LAYOUT = ((16, 0), (8, 16), (4, 24), (2, 28))
VMEM_BYTES = 20 * 1024 * 1024
WIDE_BYTES = 63 * 1024 * 1024


def split(x):
    high = x.astype(BF16)
    return high, (x - high.astype(F32)).astype(BF16)


def lanes(rows):
    return lax.broadcasted_iota(jnp.int32, (rows, 128), 1)


def table_form(table):
    high, low = split(table)
    return jnp.concatenate([high, low, high, low], axis=0)


def coef_form(packed):
    lane = lanes(packed.shape[0])
    even = 2 * (lane % 32)
    parts = [
        jnp.take_along_axis(packed, even + shift, axis=1) for shift in (0, 64, 1, 65)
    ]
    full = jnp.concatenate(parts, axis=0)
    high, low = split(full)
    return jnp.where(lanes(full.shape[0]) < 64, high.astype(F32), low.astype(F32)).astype(BF16)


def dot(a, b):
    return lax.dot_general(a, b, (((1,), (0,)), ((), ())), preferred_element_type=F32)


def dot_t(a, b):
    return lax.dot_general(a, b, (((1,), (1,)), ((), ())), preferred_element_type=F32)


def fold(out):
    rows = out.shape[0] // 4
    left = lanes(rows) < 64
    straight = jnp.where(left, out[0:rows], out[3 * rows :])
    crossed = jnp.where(left, out[rows : 2 * rows], out[2 * rows : 3 * rows])
    return straight + pltpu.roll(crossed, 64, 1)


def times(packed, table):
    return fold(dot(coef_form(packed), table_form(table)))


def row_form(packed):
    left = lanes(8) < 64
    turned = pltpu.roll(packed, 64, 1)
    zero = jnp.zeros_like(packed)
    full = jnp.concatenate(
        [
            jnp.where(left, packed, zero),
            jnp.where(left, turned, zero),
            jnp.where(left, zero, turned),
            jnp.where(left, zero, packed),
        ],
        axis=0,
    )
    return jnp.concatenate(split(full), axis=0)


def times_t_raw(rows, forms):
    out = dot_t(rows, forms)
    return out[:32] + pltpu.roll(out[:32], 96, 1) + out[32:]


def weave(raw, child):
    lane = lanes(8)
    place = 64 * child + (lane % 64) // 2
    pick = [jnp.take_along_axis(raw[8 * k : 8 * k + 8], place, axis=1) for k in range(4)]
    even = lane % 2 == 0
    return jnp.where(
        lane < 64, jnp.where(even, pick[0], pick[2]), jnp.where(even, pick[1], pick[3])
    )


def times_t(packed, table):
    return weave(times_t_raw(row_form(packed), table_form(table)), 0)


def unpack(packed):
    return jnp.concatenate([packed[:, :RANK], packed[:, RANK:]], axis=0)


def pack(value):
    return jnp.concatenate([value[:8], value[8:]], axis=1)


def place_of_device():
    device = lax.axis_index("leaf").astype(jnp.int32)
    return device, device & (GROUP - 1), device >> GROUP_BITS


def up_kernel(sources, basis, transfer, coefs, root, tables):
    table = transfer[...].reshape(LOCAL, 32, 128)
    for row in range(LOCAL):
        high, low = split(table[row])
        tables[row, 0:32] = high
        tables[row, 32:64] = low
    for leaf in range(LEAVES):
        entries = sources[:, leaf * POINTS : (leaf + 1) * POINTS]
        high, low = split(entries)
        basis_high, basis_low = split(basis[leaf])
        both = dot_t(jnp.concatenate([high, low], axis=0), basis_high)
        coefs[leaf] = pack(both[:16] + both[16:] + dot_t(high, basis_low))
    for level, (clusters, offset) in enumerate(LAYOUT):
        for parent in range(clusters // 2):
            first = offset + 2 * parent
            left = jnp.concatenate(
                [coef_form(coefs[first]), coef_form(coefs[first + 1])], axis=1
            )
            halves = [tables[first], tables[first], tables[first + 1], tables[first + 1]]
            value = fold(dot(left, jnp.concatenate(halves, axis=0)))
            if clusters > 2:
                coefs[offset + clusters + parent] = value
            else:
                root[...] = value


def edge_kernel(sources, coefs, forward, backward):
    forward[0:LOCAL] = coefs[...]
    backward[0:LOCAL] = coefs[...]
    for leaf in range(LEAVES):
        edge, place = (backward, leaf) if leaf < REACH else (forward, leaf - REACH)
        entries = sources[:, leaf * POINTS : (leaf + 1) * POINTS]
        edge[LOCAL + 2 * place] = entries[:8]
        edge[LOCAL + 2 * place + 1] = entries[8:]


def group_sums(sibling, raw, table, out):
    terms = [
        times(sibling[level], table[2 * GROUP_BITS - 2 - level]) for level in range(GROUP_BITS)
    ]
    value = terms[GROUP_BITS - 1]
    product = raw[0]
    for level in range(GROUP_BITS - 2, -1, -1):
        value = times_t(value, raw[0] if level == 0 else table[level - 1]) + terms[level]
    for level in range(1, GROUP_BITS):
        product = times(product, table[level - 1])
    out[NEAR_ROWS : NEAR_ROWS + 8] = value
    out[NEAR_ROWS + 8 : NEAR_ROWS + 40] = product


def near_kernel(partner, count, own, low, high, block, sibling, raw, table, out, leaves):
    group_sums(sibling, raw, table, out)
    for leaf in range(LEAVES):
        leaves[REACH + leaf] = own[:, leaf * POINTS : (leaf + 1) * POINTS]
    for leaf in range(REACH):
        for half in range(2):
            rows = slice(8 * half, 8 * half + 8)
            leaves[leaf, rows] = low[LOCAL + 2 * leaf + half]
            leaves[REACH + LEAVES + leaf, rows] = high[LOCAL + 2 * leaf + half]
    first = place_of_device()[0] * LEAVES - REACH
    for leaf in range(LEAVES):
        total = None
        for slot in range(NEAR):
            place = jnp.clip(partner[slot, leaf] - first, 0, LEAVES + 2 * REACH - 1)
            used = (slot < count[leaf]).astype(F32)
            picked_high, picked_low = split(leaves[place] * used)
            block_high, block_low = split(block[leaf, slot])
            both = dot_t(jnp.concatenate([picked_high, picked_low], axis=0), block_high)
            value = both[:16] + both[16:] + dot_t(picked_high, block_low)
            total = value if total is None else total + value
        out[16 * leaf : 16 * leaf + 16] = total


def top_sums(low, upper, sums, out):
    value = times(sums[2], upper[3])
    value = times_t(value, low[2]) + times(sums[1], low[1])
    out[0:8] = times_t(value, low[4]) + times(sums[0], low[3])
    out[8:40] = times(times(low[4], low[2]), low[0])
    for entry in range(3):
        out[40 + 32 * entry : 72 + 32 * entry] = upper[entry]


def far_kernel(
    partner, count, own, low, high, coupling, low_table, upper, sums, out, prepared, extended
):
    top_sums(low_table, upper, sums, prepared)
    device = place_of_device()[0]
    extended[0:LOCAL] = low[0:LOCAL]
    extended[LOCAL : 2 * LOCAL] = own[...]
    extended[2 * LOCAL : 3 * LOCAL] = high[0:LOCAL]
    tables = [coupling[slot].reshape(LOCAL, 32, 128) for slot in range(SLOTS)]
    for clusters, offset in LAYOUT:
        for cluster in range(clusters):
            row = offset + cluster
            left = []
            right = []
            for slot in range(SLOTS):
                index = partner[slot, row]
                side = jnp.clip(index // clusters - device + 1, 0, 2)
                place = side * LOCAL + offset + index % clusters
                used = (slot < count[row]).astype(F32)
                left.append(coef_form(extended[place] * used))
                right.append(table_form(tables[slot][row]))
            out[row] = fold(dot(jnp.concatenate(left, axis=1), jnp.concatenate(right, axis=0)))


def call(kernel, name, outs, args, lazy=(), scalars=0, scratch=(), after=(), flops=0):
    vmem = pl.BlockSpec(memory_space=pltpu.VMEM)
    smem = pl.BlockSpec(memory_space=pltpu.SMEM)
    spare = pl.BlockSpec(memory_space=pl.ANY)
    given, slow, spares = len(args), len(lazy), len(after)

    def body(*refs):
        own = refs[given + slow + spares :]
        copies = []
        getters = []
        if slow:
            own, targets, semaphores = own[: -slow - 1], own[-slow - 1 : -1], own[-1]
            for i, target in enumerate(targets):
                copies.append(
                    pltpu.make_async_copy(refs[given + i], target, semaphores.at[i])
                )
                copies[-1].start()
            waiting = set(range(slow))

            def getter(i):
                def get():
                    if i in waiting:
                        waiting.remove(i)
                        copies[i].wait()
                    return targets[i]

                return get

            getters = [getter(i) for i in range(slow)]
        kernel(*refs[:given], *getters, *own)
        for get in getters:
            get()

    buffers = [pltpu.VMEM(item.shape, item.dtype) for item in lazy]
    if lazy:
        buffers.append(pltpu.SemaphoreType.DMA((slow,)))
    result = pl.pallas_call(
        body,
        out_shape=list(outs),
        in_specs=[smem] * scalars + [vmem] * (given - scalars) + [spare] * (slow + spares),
        out_specs=[vmem] * len(outs),
        scratch_shapes=list(scratch) + buffers,
        compiler_params=pltpu.CompilerParams(
            vmem_limit_bytes=WIDE_BYTES if lazy else VMEM_BYTES
        ),
        cost_estimate=pl.CostEstimate(
            flops=flops, bytes_accessed=flops // 400, transcendentals=0
        ),
        name=name,
    )(*args, *lazy, *after)
    return result if len(result) > 1 else result[0]


def shape(*dims, dtype=F32):
    return jax.ShapeDtypeStruct(dims, dtype)


def permute(value, pairs):
    return lax.ppermute(value, "leaf", pairs)


def tables(size):
    return shape(size, 32, 128)


def prepare_kernel(transfers, couplings, group_raw, top_raw, group_pay):
    def coupling(level, side):
        return couplings[level - 1, :, side, :]

    group_pay[0] = coupling(GROUP_BITS, 1)
    top_raw[0:3] = transfers[4:7]
    top_raw[HIGH] = transfers[7]
    for side in range(2):
        for level in range(7, 10):
            top_raw[HIGH + 1 + 3 * side + level - 7] = coupling(level, side)
        for level in range(5, 7):
            top_raw[3 + 2 * side + level - 5] = coupling(level, side)
        for level in range(1, 5):
            group_raw[4 + 4 * side + level - 1] = coupling(level, side)
    group_raw[0:4] = transfers[0:4]


def choose(flag, first, second):
    return jnp.where(flag, first, second)


def merge_group(raw, bit, live, arrived, out):
    _, member, _ = place_of_device()
    right_child = ((member >> bit) & 1) == 1
    size = out.shape[0]
    start = 0
    if bit + 1 < GROUP_BITS:
        out[0] = choose(right_child, arrived[0], raw[bit + 1])
        start = 1
    for entry in range(start, size - 1):
        out[entry] = choose(right_child, arrived[entry], live[entry - start])
    out[size - 1] = choose(right_child, arrived[size - 1], raw[GROUP_BITS + bit])


def group_payload(raw, bit, live, pay):
    pay[0] = raw[bit + 1]
    size = live.shape[0]
    pay[1 : 1 + size] = live[...]
    pay[1 + size] = raw[2 * GROUP_BITS + bit]


def first_kernel(raw, arrived, top_raw, live, pay):
    merge_group(raw, 3, None, arrived, live)
    group_payload(raw, 2, live, pay)

    @pl.when(place_of_device()[1] == PORTER)
    def _():
        pay[0] = top_raw[HIGH + 6]


def second_kernel(raw, arrived, live, top_raw, out, pay, ninth):
    merge_group(raw, 2, live, arrived, out)
    group_payload(raw, 1, out, pay)
    _, member, group = place_of_device()
    value = choose(((group >> 4) & 1) == 1, arrived[0], top_raw[HIGH + 3])
    ninth[0] = value

    @pl.when(member == PORTER)
    def _():
        pay[0] = value
        pay[1] = top_raw[HIGH + 5]


def third_kernel(raw, arrived, live, top_raw, ninth, out, pay, upper, near_pay, far_pay):
    merge_group(raw, 1, live, arrived, out)
    group_payload(raw, 0, out, pay)
    _, _, group = place_of_device()
    right_child = ((group >> 3) & 1) == 1
    values = (
        top_raw[HIGH],
        choose(right_child, arrived[0], ninth[0]),
        choose(right_child, arrived[1], top_raw[HIGH + 2]),
    )
    for target, side in ((upper, 1), (near_pay, 1), (far_pay, 4)):
        for entry in range(3):
            target[entry] = values[entry]
        target[3] = top_raw[HIGH + side]
    near_pay[4] = top_raw[2]
    near_pay[5] = top_raw[6]


def fourth_kernel(top_raw, upper, near_in, far_in, out, keep, low_pay):
    _, _, group = place_of_device()
    place = group & 7
    for entry in range(4):
        out[entry] = choose(
            place == 2, near_in[entry], choose(place == 6, far_in[entry], upper[entry])
        )
    second = ((group >> 1) & 1) == 1
    sixth = choose(second, near_in[4], top_raw[2])
    coupling = choose(second, near_in[5], top_raw[4])
    for target, side in ((keep, 3), (low_pay, 5)):
        target[0] = sixth
        target[1] = coupling
        target[2] = top_raw[1]
        target[3] = top_raw[side]
    keep[4] = top_raw[0]


def share_kernel(root, raw, live, arrived, blocks, table, chain):
    _, member, _ = place_of_device()
    merge_group(raw, 0, live, arrived, table)
    value = root[...]
    chain[0] = value
    for level in range(GROUP_BITS):
        value = times(value, raw[0] if level == 0 else table[level - 1])
        if level + 1 < GROUP_BITS:
            chain[level + 1] = value
    for other in range(GROUP):
        apart = member ^ other
        level = sum((apart >= (1 << bit)).astype(jnp.int32) for bit in range(1, GROUP_BITS))
        blocks[other, 0:8] = chain[level]
        blocks[other, 8:16] = value


def total_of(pieces):
    total = pieces[0]
    for piece in pieces[1:]:
        total = total + piece
    return total


def rise_kernel(given, keep, near_in, blocks, sibling, table, chain):
    _, member, group = place_of_device()
    place = group & 7
    odd = (place & 1) == 1
    for entry in range(4):
        table[entry] = choose(odd, near_in[entry], keep[entry])
    table[4] = keep[4]
    for level in range(GROUP_BITS):
        sibling[level] = total_of(
            [given[member ^ apart, 0:8] for apart in range(1 << level, 2 << level)]
        )
    value = total_of([given[other, 8:16] for other in range(GROUP)])
    chain[0] = value
    for level in range(3):
        value = times(value, table[4 - 2 * level])
        chain[level + 1] = value
    for other in range(8):
        apart = place ^ other
        level = sum((apart >= (1 << bit)).astype(jnp.int32) for bit in range(1, 3))
        blocks[other, 0:8] = chain[level]
        blocks[other, 8:16] = value


def fifth_kernel(upper, near_in, far_in, next_in, out):
    _, _, group = place_of_device()
    place = group & 7
    for entry in range(4):
        even = choose(place == 4, far_in[entry], upper[entry])
        odd = choose(place == 5, next_in[entry], near_in[entry])
        out[entry] = choose((place & 1) == 1, odd, even)


def middle_kernel(given, upper, blocks, sums):
    _, _, group = place_of_device()
    place, line = group & 7, group >> 3
    for level in range(3):
        sums[level] = total_of(
            [given[place ^ apart, 0:8] for apart in range(1 << level, 2 << level)]
        )
    value = total_of([given[other, 8:16] for other in range(8)])
    raised = times(value, upper[0])
    for other in range(4):
        blocks[other] = choose((line ^ other) >= 2, raised, value)


def turn_kernel(given, prepared, out):
    _, _, group = place_of_device()
    line = group >> 3
    seventh = times(given[line ^ 1], prepared[104:136])
    eighth = times(given[line ^ 2] + given[line ^ 3], prepared[72:104])
    value = times_t(eighth, prepared[40:72]) + seventh
    value = times_t(value, prepared[8:40]) + prepared[0:8]
    for other in range(GROUP):
        out[other] = value


def down_kernel(given, near, forms, far, basis, out):
    near = near()
    value = times_t(given[PORTER], near[NEAR_ROWS + 8 : NEAR_ROWS + 40])
    value = value + near[NEAR_ROWS : NEAR_ROWS + 8]
    parents = [value]
    forms, far = forms(), far()
    for clusters, offset in reversed(LAYOUT):
        following = []
        for parent in range(clusters // 2):
            first = offset + 2 * parent
            pair = jnp.concatenate([forms[first], forms[first + 1]], axis=0)
            raw = times_t_raw(row_form(parents[parent]), pair)
            following.append(weave(raw, 0) + far[first])
            following.append(weave(raw, 1) + far[first + 1])
        parents = following
    basis = basis()
    for leaf in range(LEAVES):
        high, low = split(unpack(parents[leaf]))
        basis_high, basis_low = split(basis[leaf])
        both = dot(jnp.concatenate([high, low], axis=0), basis_high)
        place = slice(leaf * POINTS, (leaf + 1) * POINTS)
        out[:, place] = both[:16] + both[16:] + dot(high, basis_low) + near[16 * leaf : 16 * leaf + 16]


def on_device(
    sources,
    leaf_cluster_basis,
    local_transfer,
    far_coupling,
    far_partner,
    far_count,
    top_transfer,
    top_coupling,
    near_block,
    near_partner,
    near_count,
):
    count = lax.axis_size("leaf")
    forward = [(i, i + 1) for i in range(count - 1)]
    backward = [(i + 1, i) for i in range(count - 1)]

    def handed(value, period, first, second):
        return permute(value, [(i + first, i + second) for i in range(0, count, period)])

    transfers = top_transfer.reshape(TOP_BITS, 32, 128)
    couplings = top_coupling.reshape(TOP_BITS, 2, 32, 128).transpose(0, 2, 1, 3)
    raw, top_raw, pay = call(
        prepare_kernel,
        "top_tables",
        [tables(12), tables(14), tables(1)],
        [transfers, couplings],
        flops=1 << 30,
    )
    group_in = handed(pay, 16, 0, 8)
    top_raw = handed(top_raw, GROUP, 0, PORTER)

    coefs, root, forms = call(
        up_kernel,
        "upward",
        [
            shape(LOCAL, 8, 128),
            shape(8, 128),
            shape(LOCAL, 64, 128, dtype=BF16),
        ],
        [sources, leaf_cluster_basis, local_transfer],
        flops=2 << 30,
    )
    live, pay = call(
        first_kernel,
        "hand_down_1",
        [tables(1), tables(3)],
        [raw, group_in, top_raw],
        flops=1 << 29,
    )
    pairs = [(i, i + 4) for i in range(0, count, 8)] + [(PORTER, 256 + PORTER)]
    group_in = permute(pay, pairs)
    live, pay, ninth = call(
        second_kernel,
        "hand_down_2",
        [tables(3), tables(5), tables(1)],
        [raw, group_in, live, top_raw],
        after=[root],
        flops=1 << 29,
    )
    pairs = [(i, i + 2) for i in range(0, count, 4)]
    pairs += [(i + PORTER, i + 128 + PORTER) for i in range(0, count, 256)]
    group_in = permute(pay, pairs)
    live, pay, upper, near_pay, far_pay = call(
        third_kernel,
        "hand_down_3",
        [tables(5), tables(7), tables(4), tables(6), tables(4)],
        [raw, group_in, live, top_raw, ninth],
        flops=1 << 29,
    )
    group_in = handed(pay, 2, 0, 1)
    near_in = handed(near_pay, 64, PORTER, 32 + PORTER)
    far_in = handed(far_pay, 128, PORTER, 96 + PORTER)
    upper, keep, low_pay = call(
        fourth_kernel,
        "hand_down_4",
        [tables(4), tables(5), tables(4)],
        [top_raw, upper, near_in, far_in],
        flops=1 << 29,
    )
    low_in = handed(low_pay, 32, PORTER, 16 + PORTER)
    near_in = handed(upper, 32, PORTER, 16 + PORTER)
    far_in = handed(upper, 128, 96 + PORTER, 64 + PORTER)
    next_in = handed(upper, 128, 96 + PORTER, 80 + PORTER)
    shares, group_table = call(
        share_kernel,
        "group_shares",
        [shape(GROUP, 16, 128), tables(7)],
        [root, raw, live, group_in],
        scratch=[pltpu.VMEM((GROUP_BITS, 8, 128), F32)],
        after=[keep],
        flops=2 << 30,
    )
    in_group = [list(range(first, first + GROUP)) for first in range(0, count, GROUP)]
    in_column = [
        list(range(line + member, line + 128, GROUP))
        for line in range(0, count, 128)
        for member in range(GROUP)
    ]
    in_line = [list(range(first, count, 128)) for first in range(128)]
    given = lax.all_to_all(shares, "leaf", 0, 0, axis_index_groups=in_group)
    upper = call(
        fifth_kernel,
        "hand_down_5",
        [tables(4)],
        [upper, near_in, far_in, next_in],
        after=[shares],
        flops=1 << 29,
    )
    blocks, sibling, low_table = call(
        rise_kernel,
        "column_shares",
        [shape(8, 16, 128), shape(GROUP_BITS, 8, 128), tables(5)],
        [given, keep, low_in],
        scratch=[pltpu.VMEM((4, 8, 128), F32)],
        flops=2 << 30,
    )
    given = lax.all_to_all(blocks, "leaf", 0, 0, axis_index_groups=in_column)
    low_edge, high_edge = call(
        edge_kernel,
        "edges",
        [shape(LOCAL + 2 * REACH, 8, 128)] * 2,
        [sources, coefs],
        after=[blocks],
        flops=1 << 29,
    )
    low_edge = permute(low_edge, forward)
    high_edge = permute(high_edge, backward)
    blocks, sums = call(
        middle_kernel,
        "line_shares",
        [shape(4, 8, 128), shape(3, 8, 128)],
        [given, upper],
        flops=1 << 30,
    )
    given = lax.all_to_all(blocks, "leaf", 0, 0, axis_index_groups=in_line)

    near = call(
        near_kernel,
        "near_field",
        [shape(NEAR_ROWS + 40, 128)],
        [
            near_partner.T,
            near_count,
            sources,
            low_edge,
            high_edge,
            near_block,
            sibling,
            raw,
            group_table,
        ],
        scalars=2,
        scratch=[pltpu.VMEM((LEAVES + 2 * REACH, 16, POINTS), F32)],
        flops=2 << 30,
    )
    far, prepared = call(
        far_kernel,
        "far_field",
        [shape(LOCAL, 8, 128), shape(136, 128)],
        [
            far_partner.T,
            far_count,
            coefs,
            low_edge,
            high_edge,
            far_coupling.transpose(1, 0, 2),
            low_table,
            upper,
            sums,
        ],
        scalars=2,
        scratch=[pltpu.VMEM((3 * LOCAL, 8, 128), F32)],
        flops=2 << 30,
    )
    turned = call(
        turn_kernel,
        "top_turn",
        [shape(GROUP, 8, 128)],
        [given, prepared],
        flops=2 << 30,
    )
    given = lax.all_to_all(turned, "leaf", 0, 0, axis_index_groups=in_group)
    return call(
        down_kernel,
        "downward",
        [shape(16, LEAVES * POINTS)],
        [given],
        lazy=[near, forms, far, leaf_cluster_basis],
        flops=4 << 30,
    )


def solution(mesh):
    placed = (
        P(None, "leaf"),
        P("leaf", None, None),
        P("leaf", None),
        P("leaf", None, None),
        P("leaf", None),
        P("leaf"),
        P("leaf", None, None),
        P("leaf", None, None, None),
        P("leaf", None, None, None),
        P("leaf", None),
        P("leaf"),
    )
    return jax.shard_map(
        on_device, mesh=mesh, in_specs=placed, out_specs=P(None, "leaf"), check_vma=False
    )
```

```python
import jax
import jax.numpy as jnp
from jax import lax
from jax.experimental import pallas as pl
from jax.experimental.pallas import tpu as pltpu
from jax.sharding import PartitionSpec as P

F32 = jnp.float32
BF16 = jnp.bfloat16
RANK = 64
LEAVES = 16
POINTS = 128
LOCAL = 30
SLOTS = 3
NEAR = 2
REACH = 8
GROUP_BITS = 4
TOP_BITS = 9
GROUP = 1 << GROUP_BITS
NEAR_ROWS = 16 * LEAVES
PORTER = 1
HIGH = 7
LAYOUT = ((16, 0), (8, 16), (4, 24), (2, 28))
VMEM_BYTES = 20 * 1024 * 1024
WIDE_BYTES = 63 * 1024 * 1024


def split(x):
    high = x.astype(BF16)
    return high, (x - high.astype(F32)).astype(BF16)


def lanes(rows):
    return lax.broadcasted_iota(jnp.int32, (rows, 128), 1)


def table_form(table):
    high, low = split(table)
    return jnp.concatenate([high, low, high, low], axis=0)


def coef_form(packed):
    lane = lanes(packed.shape[0])
    even = 2 * (lane % 32)
    parts = [
        jnp.take_along_axis(packed, even + shift, axis=1) for shift in (0, 64, 1, 65)
    ]
    full = jnp.concatenate(parts, axis=0)
    high, low = split(full)
    return jnp.where(lanes(full.shape[0]) < 64, high.astype(F32), low.astype(F32)).astype(BF16)


def dot(a, b):
    return lax.dot_general(a, b, (((1,), (0,)), ((), ())), preferred_element_type=F32)


def dot_t(a, b):
    return lax.dot_general(a, b, (((1,), (1,)), ((), ())), preferred_element_type=F32)


def fold(out):
    rows = out.shape[0] // 4
    left = lanes(rows) < 64
    straight = jnp.where(left, out[0:rows], out[3 * rows :])
    crossed = jnp.where(left, out[rows : 2 * rows], out[2 * rows : 3 * rows])
    return straight + pltpu.roll(crossed, 64, 1)


def times(packed, table):
    return fold(dot(coef_form(packed), table_form(table)))


def row_form(packed):
    left = lanes(packed.shape[0]) < 64
    turned = pltpu.roll(packed, 64, 1)
    zero = jnp.zeros_like(packed)
    full = jnp.concatenate(
        [
            jnp.where(left, packed, zero),
            jnp.where(left, turned, zero),
            jnp.where(left, zero, turned),
            jnp.where(left, zero, packed),
        ],
        axis=0,
    )
    return jnp.concatenate(split(full), axis=0)


def times_t_raw(rows, forms):
    out = dot_t(rows, forms)
    half = out.shape[0] // 2
    return out[:half] + pltpu.roll(out[:half], 96, 1) + out[half:]


def weave(raw, child):
    rows = raw.shape[0] // 4
    lane = lanes(rows)
    place = 64 * child + (lane % 64) // 2
    pick = [
        jnp.take_along_axis(raw[rows * k : rows * k + rows], place, axis=1) for k in range(4)
    ]
    even = lane % 2 == 0
    return jnp.where(
        lane < 64, jnp.where(even, pick[0], pick[2]), jnp.where(even, pick[1], pick[3])
    )


def times_t(packed, table):
    return weave(times_t_raw(row_form(packed), table_form(table)), 0)


def unpack(packed):
    return jnp.concatenate([packed[:, :RANK], packed[:, RANK:]], axis=0)


def pack(value):
    return jnp.concatenate([value[:8], value[8:]], axis=1)


def place_of_device():
    device = lax.axis_index("leaf").astype(jnp.int32)
    return device, device & (GROUP - 1), device >> GROUP_BITS


def up_kernel(sources, basis, transfer, coefs, root, tables):
    table = transfer[...].reshape(LOCAL, 32, 128)
    for row in range(LOCAL):
        high, low = split(table[row])
        tables[row, 0:32] = high
        tables[row, 32:64] = low
    for leaf in range(LEAVES):
        entries = sources[:, leaf * POINTS : (leaf + 1) * POINTS]
        high, low = split(entries)
        basis_high, basis_low = split(basis[leaf])
        both = dot_t(jnp.concatenate([high, low], axis=0), basis_high)
        coefs[leaf] = pack(both[:16] + both[16:] + dot_t(high, basis_low))
    for level, (clusters, offset) in enumerate(LAYOUT):
        for parent in range(clusters // 2):
            first = offset + 2 * parent
            left = jnp.concatenate(
                [coef_form(coefs[first]), coef_form(coefs[first + 1])], axis=1
            )
            halves = [tables[first], tables[first], tables[first + 1], tables[first + 1]]
            value = fold(dot(left, jnp.concatenate(halves, axis=0)))
            if clusters > 2:
                coefs[offset + clusters + parent] = value
            else:
                root[...] = value


def edge_kernel(sources, coefs, inner, outer):
    odd = (place_of_device()[0] & 1) == 1
    inner[0:LOCAL] = coefs[...]
    outer[0:LOCAL] = coefs[...]
    for place in range(REACH):
        first = sources[:, place * POINTS : (place + 1) * POINTS]
        last = sources[:, (REACH + place) * POINTS : (REACH + place + 1) * POINTS]
        for edge, value in (
            (inner, jnp.where(odd, first, last)),
            (outer, jnp.where(odd, last, first)),
        ):
            edge[LOCAL + 2 * place] = value[:8]
            edge[LOCAL + 2 * place + 1] = value[8:]


def group_sums(sibling, raw, table, out):
    terms = [
        times(sibling[level], table[2 * GROUP_BITS - 2 - level]) for level in range(GROUP_BITS)
    ]
    value = terms[GROUP_BITS - 1]
    product = raw[0]
    for level in range(GROUP_BITS - 2, -1, -1):
        value = times_t(value, raw[0] if level == 0 else table[level - 1]) + terms[level]
    for level in range(1, GROUP_BITS):
        product = times(product, table[level - 1])
    out[NEAR_ROWS : NEAR_ROWS + 8] = value
    out[NEAR_ROWS + 8 : NEAR_ROWS + 40] = product


def near_kernel(partner, count, own, inner, outer, block, sibling, raw, table, out, leaves):
    group_sums(sibling, raw, table, out)
    odd = (place_of_device()[0] & 1) == 1
    for leaf in range(LEAVES):
        leaves[REACH + leaf] = own[:, leaf * POINTS : (leaf + 1) * POINTS]
    for leaf in range(REACH):
        for half in range(2):
            rows = slice(8 * half, 8 * half + 8)
            place = LOCAL + 2 * leaf + half
            leaves[leaf, rows] = jnp.where(odd, inner[place], outer[place])
            leaves[REACH + LEAVES + leaf, rows] = jnp.where(odd, outer[place], inner[place])
    first = place_of_device()[0] * LEAVES - REACH
    for leaf in range(LEAVES):
        total = None
        for slot in range(NEAR):
            place = jnp.clip(partner[slot, leaf] - first, 0, LEAVES + 2 * REACH - 1)
            used = (slot < count[leaf]).astype(F32)
            picked_high, picked_low = split(leaves[place] * used)
            block_high, block_low = split(block[leaf, slot])
            both = dot_t(jnp.concatenate([picked_high, picked_low], axis=0), block_high)
            value = both[:16] + both[16:] + dot_t(picked_high, block_low)
            total = value if total is None else total + value
        out[16 * leaf : 16 * leaf + 16] = total


def top_sums(low, upper, sums, out):
    second_half = ((place_of_device()[2] >> 2) & 1) == 1
    value = times(sums[2], choose(second_half, upper[4], upper[3]))
    value = times_t(value, low[2]) + times(sums[1], low[1])
    out[0:8] = times_t(value, low[4]) + times(sums[0], low[3])
    out[8:40] = times(times(low[4], low[2]), low[0])
    for entry in range(3):
        out[40 + 32 * entry : 72 + 32 * entry] = upper[entry]


def far_kernel(
    partner, count, own, inner, outer, coupling, low_table, upper, sums, out, prepared, extended
):
    top_sums(low_table, upper, sums, prepared)
    device = place_of_device()[0]
    odd = (device & 1) == 1
    extended[0:LOCAL] = jnp.where(odd, inner[0:LOCAL], outer[0:LOCAL])
    extended[LOCAL : 2 * LOCAL] = own[...]
    extended[2 * LOCAL : 3 * LOCAL] = jnp.where(odd, outer[0:LOCAL], inner[0:LOCAL])
    tables = [coupling[slot].reshape(LOCAL, 32, 128) for slot in range(SLOTS)]
    for clusters, offset in LAYOUT:
        for cluster in range(clusters):
            row = offset + cluster
            left = []
            right = []
            for slot in range(SLOTS):
                index = partner[slot, row]
                side = jnp.clip(index // clusters - device + 1, 0, 2)
                place = side * LOCAL + offset + index % clusters
                used = (slot < count[row]).astype(F32)
                left.append(coef_form(extended[place] * used))
                right.append(table_form(tables[slot][row]))
            out[row] = fold(dot(jnp.concatenate(left, axis=1), jnp.concatenate(right, axis=0)))


def call(kernel, name, outs, args, lazy=(), scalars=0, scratch=(), after=(), flops=0):
    vmem = pl.BlockSpec(memory_space=pltpu.VMEM)
    smem = pl.BlockSpec(memory_space=pltpu.SMEM)
    spare = pl.BlockSpec(memory_space=pl.ANY)
    given, slow, spares = len(args), len(lazy), len(after)

    def body(*refs):
        own = refs[given + slow + spares :]
        copies = []
        getters = []
        if slow:
            own, targets, semaphores = own[: -slow - 1], own[-slow - 1 : -1], own[-1]
            for i, target in enumerate(targets):
                copies.append(
                    pltpu.make_async_copy(refs[given + i], target, semaphores.at[i])
                )
                copies[-1].start()
            waiting = set(range(slow))

            def getter(i):
                def get():
                    if i in waiting:
                        waiting.remove(i)
                        copies[i].wait()
                    return targets[i]

                return get

            getters = [getter(i) for i in range(slow)]
        kernel(*refs[:given], *getters, *own)
        for get in getters:
            get()

    buffers = [pltpu.VMEM(item.shape, item.dtype) for item in lazy]
    if lazy:
        buffers.append(pltpu.SemaphoreType.DMA((slow,)))
    result = pl.pallas_call(
        body,
        out_shape=list(outs),
        in_specs=[smem] * scalars + [vmem] * (given - scalars) + [spare] * (slow + spares),
        out_specs=[vmem] * len(outs),
        scratch_shapes=list(scratch) + buffers,
        compiler_params=pltpu.CompilerParams(
            vmem_limit_bytes=WIDE_BYTES if lazy else VMEM_BYTES
        ),
        cost_estimate=pl.CostEstimate(
            flops=flops, bytes_accessed=flops // 400, transcendentals=0
        ),
        name=name,
    )(*args, *lazy, *after)
    return result if len(result) > 1 else result[0]


def shape(*dims, dtype=F32):
    return jax.ShapeDtypeStruct(dims, dtype)


def permute(value, pairs):
    return lax.ppermute(value, "leaf", pairs)


def tables(size):
    return shape(size, 32, 128)


def prepare_kernel(transfers, couplings, group_raw, top_raw, group_pay):
    def coupling(level, side):
        return couplings[level - 1, :, side, :]

    group_pay[0] = coupling(GROUP_BITS, 1)
    top_raw[0:3] = transfers[4:7]
    top_raw[HIGH] = transfers[7]
    for side in range(2):
        for level in range(7, 10):
            top_raw[HIGH + 1 + 3 * side + level - 7] = coupling(level, side)
        for level in range(5, 7):
            top_raw[3 + 2 * side + level - 5] = coupling(level, side)
        for level in range(1, 5):
            group_raw[4 + 4 * side + level - 1] = coupling(level, side)
    group_raw[0:4] = transfers[0:4]


def choose(flag, first, second):
    return jnp.where(flag, first, second)


def merge_group(raw, bit, live, arrived, out):
    _, member, _ = place_of_device()
    right_child = ((member >> bit) & 1) == 1
    size = out.shape[0]
    start = 0
    if bit + 1 < GROUP_BITS:
        out[0] = choose(right_child, arrived[0], raw[bit + 1])
        start = 1
    for entry in range(start, size - 1):
        out[entry] = choose(right_child, arrived[entry], live[entry - start])
    out[size - 1] = choose(right_child, arrived[size - 1], raw[GROUP_BITS + bit])


def group_payload(raw, bit, live, pay):
    pay[0] = raw[bit + 1]
    size = live.shape[0]
    pay[1 : 1 + size] = live[...]
    pay[1 + size] = raw[2 * GROUP_BITS + bit]


def first_kernel(raw, arrived, top_raw, live, pay):
    merge_group(raw, 3, None, arrived, live)
    group_payload(raw, 2, live, pay)

    @pl.when(place_of_device()[1] == PORTER)
    def _():
        pay[0] = top_raw[HIGH + 6]
        pay[1] = top_raw[HIGH]


def second_kernel(raw, arrived, live, top_raw, out, pay, ninth):
    merge_group(raw, 2, live, arrived, out)
    group_payload(raw, 1, out, pay)
    _, member, group = place_of_device()
    value = choose(((group >> 4) & 1) == 1, arrived[0], top_raw[HIGH + 3])
    ninth[0] = value
    ninth[1] = arrived[1]

    @pl.when(member == PORTER)
    def _():
        pay[0] = value
        pay[1] = top_raw[HIGH + 5]
        pay[2] = arrived[1]


def third_kernel(raw, arrived, live, top_raw, ninth, out, pay, upper, near_pay):
    merge_group(raw, 1, live, arrived, out)
    group_payload(raw, 0, out, pay)
    _, member, group = place_of_device()
    right_child = ((group >> 3) & 1) == 1
    upper[...] = jnp.zeros_like(upper)

    @pl.when((member == PORTER) & ((group & 7) == 0))
    def _():
        own = top_raw[HIGH]
        across = choose(right_child, arrived[0], ninth[0])
        upper[0] = times_t(times(ninth[1], across), own)
        upper[1] = times_t(times(arrived[2], across), own)
        upper[2] = choose(right_child, arrived[1], top_raw[HIGH + 2])

    upper[3] = top_raw[HIGH + 1]
    upper[4] = top_raw[HIGH + 4]
    near_pay[0:5] = upper[...]
    near_pay[5] = top_raw[2]
    near_pay[6] = top_raw[6]


def fourth_kernel(top_raw, upper, near_in, far_in, out, keep, low_pay):
    _, _, group = place_of_device()
    place = group & 7
    for entry in range(5):
        value = choose(
            place == 2, near_in[entry], choose(place == 6, far_in[entry], upper[entry])
        )
        out[entry] = value
        low_pay[4 + entry] = value
    second = ((group >> 1) & 1) == 1
    sixth = choose(second, near_in[5], top_raw[2])
    coupling = choose(second, near_in[6], top_raw[4])
    for target, side in ((keep, 3), (low_pay, 5)):
        target[0] = sixth
        target[1] = coupling
        target[2] = top_raw[1]
        target[3] = top_raw[side]
    keep[4] = top_raw[0]


def share_kernel(root, raw, live, arrived, blocks, table, chain):
    _, member, _ = place_of_device()
    merge_group(raw, 0, live, arrived, table)
    value = root[...]
    chain[0] = value
    for level in range(GROUP_BITS):
        value = times(value, raw[0] if level == 0 else table[level - 1])
        if level + 1 < GROUP_BITS:
            chain[level + 1] = value
    for other in range(GROUP):
        apart = member ^ other
        level = sum((apart >= (1 << bit)).astype(jnp.int32) for bit in range(1, GROUP_BITS))
        blocks[other, 0:8] = chain[level]
        blocks[other, 8:16] = value


def total_of(pieces):
    total = pieces[0]
    for piece in pieces[1:]:
        total = total + piece
    return total


def rise_kernel(given, keep, near_in, blocks, sibling, table, chain):
    _, member, group = place_of_device()
    place = group & 7
    odd = (place & 1) == 1
    for entry in range(4):
        table[entry] = choose(odd, near_in[entry], keep[entry])
    table[4] = keep[4]
    for level in range(GROUP_BITS):
        sibling[level] = total_of(
            [given[member ^ apart, 0:8] for apart in range(1 << level, 2 << level)]
        )
    value = total_of([given[other, 8:16] for other in range(GROUP)])
    chain[0] = value
    for level in range(3):
        value = times(value, table[4 - 2 * level])
        chain[level + 1] = value
    for other in range(8):
        apart = place ^ other
        level = sum((apart >= (1 << bit)).astype(jnp.int32) for bit in range(1, 3))
        blocks[other, 0:8] = chain[level]
        blocks[other, 8:16] = value


def fifth_kernel(upper, low_in, far_in, out):
    _, _, group = place_of_device()
    place = group & 7
    for entry in range(5):
        value = choose((place & 1) == 1, low_in[4 + entry], upper[entry])
        out[entry] = choose((place == 4) | (place == 5), far_in[entry], value)


def middle_kernel(given, blocks, sums):
    _, _, group = place_of_device()
    place = group & 7
    value = total_of([given[other, 8:16] for other in range(8)])
    for other in range(4):
        blocks[other] = value
    for level in range(3):
        sums[level] = total_of(
            [given[place ^ apart, 0:8] for apart in range(1 << level, 2 << level)]
        )


def turn_kernel(given, prepared, out):
    _, _, group = place_of_device()
    line = group >> 3
    left = [coef_form(given[line ^ apart]) for apart in (2, 3, 1)]
    right = [table_form(prepared[40 + 32 * entry : 72 + 32 * entry]) for entry in range(3)]
    value = fold(dot(jnp.concatenate(left, axis=1), jnp.concatenate(right, axis=0)))
    value = times_t(value, prepared[8:40]) + prepared[0:8]
    for other in range(GROUP):
        out[other] = value


def down_kernel(given, near, forms, far, basis, out):
    near = near()
    value = times_t(given[PORTER], near[NEAR_ROWS + 8 : NEAR_ROWS + 40])
    value = value + near[NEAR_ROWS : NEAR_ROWS + 8]
    parents = [value]
    forms, far = forms(), far()
    for clusters, offset in reversed(LAYOUT):
        following = []
        for parent in range(clusters // 2):
            first = offset + 2 * parent
            pair = jnp.concatenate([forms[first], forms[first + 1]], axis=0)
            raw = times_t_raw(row_form(parents[parent]), pair)
            following.append(weave(raw, 0) + far[first])
            following.append(weave(raw, 1) + far[first + 1])
        parents = following
    basis = basis()
    for leaf in range(LEAVES):
        high, low = split(unpack(parents[leaf]))
        basis_high, basis_low = split(basis[leaf])
        both = dot(jnp.concatenate([high, low], axis=0), basis_high)
        place = slice(leaf * POINTS, (leaf + 1) * POINTS)
        out[:, place] = both[:16] + both[16:] + dot(high, basis_low) + near[16 * leaf : 16 * leaf + 16]


def on_device(
    sources,
    leaf_cluster_basis,
    local_transfer,
    far_coupling,
    far_partner,
    far_count,
    top_transfer,
    top_coupling,
    near_block,
    near_partner,
    near_count,
):
    count = lax.axis_size("leaf")
    forward = [(i, i + 1) for i in range(1, count - 1, 2)]

    def handed(value, period, first, second):
        return permute(value, [(i + first, i + second) for i in range(0, count, period)])

    transfers = top_transfer.reshape(TOP_BITS, 32, 128)
    couplings = top_coupling.reshape(TOP_BITS, 2, 32, 128).transpose(0, 2, 1, 3)
    raw, top_raw, pay = call(
        prepare_kernel,
        "top_tables",
        [tables(12), tables(14), tables(1)],
        [transfers, couplings],
        flops=1 << 30,
    )
    group_in = handed(pay, 16, 0, 8)
    top_raw = handed(top_raw, GROUP, 0, PORTER)

    coefs, root, forms = call(
        up_kernel,
        "upward",
        [
            shape(LOCAL, 8, 128),
            shape(8, 128),
            shape(LOCAL, 64, 128, dtype=BF16),
        ],
        [sources, leaf_cluster_basis, local_transfer],
        flops=2 << 30,
    )
    live, pay = call(
        first_kernel,
        "hand_down_1",
        [tables(1), tables(3)],
        [raw, group_in, top_raw],
        flops=1 << 29,
    )
    pairs = [(i, i + 4) for i in range(0, count, 8)]
    pairs += [(i + PORTER, (i ^ 256) + PORTER) for i in range(0, count, 128)]
    group_in = permute(pay, pairs)
    live, pay, ninth = call(
        second_kernel,
        "hand_down_2",
        [tables(3), tables(5), tables(2)],
        [raw, group_in, live, top_raw],
        after=[root],
        flops=1 << 29,
    )
    pairs = [(i, i + 2) for i in range(0, count, 4)]
    pairs += [(i + PORTER, (i ^ 128) + PORTER) for i in range(0, count, 128)]
    group_in = permute(pay, pairs)
    live, pay, upper, near_pay = call(
        third_kernel,
        "hand_down_3",
        [tables(5), tables(7), tables(5), tables(7)],
        [raw, group_in, live, top_raw, ninth],
        flops=1 << 29,
    )
    group_in = handed(pay, 2, 0, 1)
    near_in = handed(near_pay, 64, PORTER, 32 + PORTER)
    far_in = handed(upper, 128, PORTER, 96 + PORTER)
    upper, keep, low_pay = call(
        fourth_kernel,
        "hand_down_4",
        [tables(5), tables(5), tables(9)],
        [top_raw, upper, near_in, far_in],
        flops=1 << 29,
    )
    low_in = handed(low_pay, 32, PORTER, 16 + PORTER)
    pairs = [(i + 32 + PORTER, i + 64 + PORTER) for i in range(0, count, 128)]
    pairs += [(i + 96 + PORTER, i + 80 + PORTER) for i in range(0, count, 128)]
    far_in = permute(upper, pairs)
    shares, group_table = call(
        share_kernel,
        "group_shares",
        [shape(GROUP, 16, 128), tables(7)],
        [root, raw, live, group_in],
        scratch=[pltpu.VMEM((GROUP_BITS, 8, 128), F32)],
        after=[keep],
        flops=2 << 30,
    )
    in_group = [list(range(first, first + GROUP)) for first in range(0, count, GROUP)]
    in_column = [
        list(range(line + member, line + 128, GROUP))
        for line in range(0, count, 128)
        for member in range(GROUP)
    ]
    in_line = [list(range(first, count, 128)) for first in range(128)]
    given = lax.all_to_all(shares, "leaf", 0, 0, axis_index_groups=in_group)
    blocks, sibling, low_table = call(
        rise_kernel,
        "column_shares",
        [shape(8, 16, 128), shape(GROUP_BITS, 8, 128), tables(5)],
        [given, keep, low_in],
        scratch=[pltpu.VMEM((4, 8, 128), F32)],
        flops=2 << 30,
    )
    given = lax.all_to_all(blocks, "leaf", 0, 0, axis_index_groups=in_column)
    inner, outer = call(
        edge_kernel,
        "edges",
        [shape(LOCAL + 2 * REACH, 8, 128)] * 2,
        [sources, coefs],
        after=[blocks],
        flops=1 << 29,
    )
    inner = permute(inner, [(i, i ^ 1) for i in range(count)])
    outer = permute(outer, forward + [(second, first) for first, second in forward])
    blocks, sums = call(
        middle_kernel,
        "line_shares",
        [shape(4, 8, 128), shape(3, 8, 128)],
        [given],
        flops=1 << 30,
    )
    upper = call(
        fifth_kernel,
        "hand_down_5",
        [tables(5)],
        [upper, low_in, far_in],
        after=[blocks],
        flops=1 << 29,
    )
    given = lax.all_to_all(blocks, "leaf", 0, 0, axis_index_groups=in_line)

    near = call(
        near_kernel,
        "near_field",
        [shape(NEAR_ROWS + 40, 128)],
        [
            near_partner.T,
            near_count,
            sources,
            inner,
            outer,
            near_block,
            sibling,
            raw,
            group_table,
        ],
        scalars=2,
        scratch=[pltpu.VMEM((LEAVES + 2 * REACH, 16, POINTS), F32)],
        flops=2 << 30,
    )
    far, prepared = call(
        far_kernel,
        "far_field",
        [shape(LOCAL, 8, 128), shape(136, 128)],
        [
            far_partner.T,
            far_count,
            coefs,
            inner,
            outer,
            far_coupling.transpose(1, 0, 2),
            low_table,
            upper,
            sums,
        ],
        scalars=2,
        scratch=[pltpu.VMEM((3 * LOCAL, 8, 128), F32)],
        flops=2 << 30,
    )
    turned = call(
        turn_kernel,
        "top_turn",
        [shape(GROUP, 8, 128)],
        [given, prepared],
        flops=2 << 30,
    )
    given = lax.all_to_all(turned, "leaf", 0, 0, axis_index_groups=in_group)
    return call(
        down_kernel,
        "downward",
        [shape(16, LEAVES * POINTS)],
        [given],
        lazy=[near, forms, far, leaf_cluster_basis],
        flops=4 << 30,
    )


def solution(mesh):
    placed = (
        P(None, "leaf"),
        P("leaf", None, None),
        P("leaf", None),
        P("leaf", None, None),
        P("leaf", None),
        P("leaf"),
        P("leaf", None, None),
        P("leaf", None, None, None),
        P("leaf", None, None, None),
        P("leaf", None),
        P("leaf"),
    )
    return jax.shard_map(
        on_device, mesh=mesh, in_specs=placed, out_specs=P(None, "leaf"), check_vma=False
    )
```

```python
import jax
import jax.numpy as jnp
from jax import lax
from jax.experimental import pallas as pl
from jax.experimental.pallas import tpu as pltpu
from jax.sharding import PartitionSpec as P

F32 = jnp.float32
BF16 = jnp.bfloat16
RANK = 64
LEAVES = 16
POINTS = 128
LOCAL = 30
SLOTS = 3
NEAR = 2
REACH = 8
GROUP_BITS = 4
TOP_BITS = 9
GROUP = 1 << GROUP_BITS
NEAR_ROWS = 16 * LEAVES
PORTER = 1
HIGH = 7
LAYOUT = ((16, 0), (8, 16), (4, 24), (2, 28))
VMEM_BYTES = 20 * 1024 * 1024
WIDE_BYTES = 63 * 1024 * 1024


def split(x):
    high = x.astype(BF16)
    return high, (x - high.astype(F32)).astype(BF16)


def lanes(rows):
    return lax.broadcasted_iota(jnp.int32, (rows, 128), 1)


def table_form(table):
    high, low = split(table)
    return jnp.concatenate([high, low, high, low], axis=0)


def coef_form(packed):
    lane = lanes(packed.shape[0])
    even = 2 * (lane % 32)
    parts = [
        jnp.take_along_axis(packed, even + shift, axis=1) for shift in (0, 64, 1, 65)
    ]
    full = jnp.concatenate(parts, axis=0)
    high, low = split(full)
    return jnp.where(lanes(full.shape[0]) < 64, high.astype(F32), low.astype(F32)).astype(BF16)


def dot(a, b):
    return lax.dot_general(a, b, (((1,), (0,)), ((), ())), preferred_element_type=F32)


def dot_t(a, b):
    return lax.dot_general(a, b, (((1,), (1,)), ((), ())), preferred_element_type=F32)


def fold(out):
    rows = out.shape[0] // 4
    left = lanes(rows) < 64
    straight = jnp.where(left, out[0:rows], out[3 * rows :])
    crossed = jnp.where(left, out[rows : 2 * rows], out[2 * rows : 3 * rows])
    return straight + pltpu.roll(crossed, 64, 1)


def times(packed, table):
    return fold(dot(coef_form(packed), table_form(table)))


def row_form(packed):
    left = lanes(packed.shape[0]) < 64
    turned = pltpu.roll(packed, 64, 1)
    zero = jnp.zeros_like(packed)
    full = jnp.concatenate(
        [
            jnp.where(left, packed, zero),
            jnp.where(left, turned, zero),
            jnp.where(left, zero, turned),
            jnp.where(left, zero, packed),
        ],
        axis=0,
    )
    return jnp.concatenate(split(full), axis=0)


def times_t_raw(rows, forms):
    out = dot_t(rows, forms)
    half = out.shape[0] // 2
    return out[:half] + pltpu.roll(out[:half], 96, 1) + out[half:]


def weave(raw, child):
    rows = raw.shape[0] // 4
    lane = lanes(rows)
    place = 64 * child + (lane % 64) // 2
    pick = [
        jnp.take_along_axis(raw[rows * k : rows * k + rows], place, axis=1) for k in range(4)
    ]
    even = lane % 2 == 0
    return jnp.where(
        lane < 64, jnp.where(even, pick[0], pick[2]), jnp.where(even, pick[1], pick[3])
    )


def times_t(packed, table):
    return weave(times_t_raw(row_form(packed), table_form(table)), 0)


def unpack(packed):
    return jnp.concatenate([packed[:, :RANK], packed[:, RANK:]], axis=0)


def pack(value):
    return jnp.concatenate([value[:8], value[8:]], axis=1)


def place_of_device():
    device = lax.axis_index("leaf").astype(jnp.int32)
    return device, device & (GROUP - 1), device >> GROUP_BITS


def up_kernel(sources, basis, transfer, coefs, root, tables):
    table = transfer[...].reshape(LOCAL, 32, 128)
    for row in range(LOCAL):
        high, low = split(table[row])
        tables[row, 0:32] = high
        tables[row, 32:64] = low
    for leaf in range(LEAVES):
        entries = sources[:, leaf * POINTS : (leaf + 1) * POINTS]
        high, low = split(entries)
        basis_high, basis_low = split(basis[leaf])
        both = dot_t(jnp.concatenate([high, low], axis=0), basis_high)
        coefs[leaf] = pack(both[:16] + both[16:] + dot_t(high, basis_low))
    for level, (clusters, offset) in enumerate(LAYOUT):
        for parent in range(clusters // 2):
            first = offset + 2 * parent
            left = jnp.concatenate(
                [coef_form(coefs[first]), coef_form(coefs[first + 1])], axis=1
            )
            halves = [tables[first], tables[first], tables[first + 1], tables[first + 1]]
            value = fold(dot(left, jnp.concatenate(halves, axis=0)))
            if clusters > 2:
                coefs[offset + clusters + parent] = value
            else:
                root[...] = value


def edge_kernel(sources, coefs, inner, outer):
    odd = (place_of_device()[0] & 1) == 1
    inner[0:LOCAL] = coefs[...]
    outer[0:LOCAL] = coefs[...]
    for place in range(REACH):
        first = sources[:, place * POINTS : (place + 1) * POINTS]
        last = sources[:, (REACH + place) * POINTS : (REACH + place + 1) * POINTS]
        for edge, value in (
            (inner, jnp.where(odd, first, last)),
            (outer, jnp.where(odd, last, first)),
        ):
            edge[LOCAL + 2 * place] = value[:8]
            edge[LOCAL + 2 * place + 1] = value[8:]


def group_sums(sibling, raw, table, out):
    terms = [
        times(sibling[level], table[2 * GROUP_BITS - 2 - level]) for level in range(GROUP_BITS)
    ]
    value = terms[GROUP_BITS - 1]
    product = raw[0]
    for level in range(GROUP_BITS - 2, -1, -1):
        value = times_t(value, raw[0] if level == 0 else table[level - 1]) + terms[level]
    for level in range(1, GROUP_BITS):
        product = times(product, table[level - 1])
    out[NEAR_ROWS : NEAR_ROWS + 8] = value
    out[NEAR_ROWS + 8 : NEAR_ROWS + 40] = product


def near_kernel(partner, count, own, inner, outer, block, sibling, raw, table, out, leaves):
    group_sums(sibling, raw, table, out)
    odd = (place_of_device()[0] & 1) == 1
    for leaf in range(LEAVES):
        leaves[REACH + leaf] = own[:, leaf * POINTS : (leaf + 1) * POINTS]
    for leaf in range(REACH):
        for half in range(2):
            rows = slice(8 * half, 8 * half + 8)
            place = LOCAL + 2 * leaf + half
            leaves[leaf, rows] = jnp.where(odd, inner[place], outer[place])
            leaves[REACH + LEAVES + leaf, rows] = jnp.where(odd, outer[place], inner[place])
    first = place_of_device()[0] * LEAVES - REACH
    for leaf in range(LEAVES):
        total = None
        for slot in range(NEAR):
            place = jnp.clip(partner[slot, leaf] - first, 0, LEAVES + 2 * REACH - 1)
            used = (slot < count[leaf]).astype(F32)
            picked_high, picked_low = split(leaves[place] * used)
            block_high, block_low = split(block[leaf, slot])
            both = dot_t(jnp.concatenate([picked_high, picked_low], axis=0), block_high)
            value = both[:16] + both[16:] + dot_t(picked_high, block_low)
            total = value if total is None else total + value
        out[16 * leaf : 16 * leaf + 16] = total


def top_sums(low, upper, sums, out):
    second_half = ((place_of_device()[2] >> 2) & 1) == 1
    value = times(sums[2], choose(second_half, upper[4], upper[3]))
    value = times_t(value, low[2]) + times(sums[1], low[1])
    out[0:8] = times_t(value, low[4]) + times(sums[0], low[3])
    out[8:40] = times(times(low[4], low[2]), low[0])
    for entry in range(3):
        out[40 + 32 * entry : 72 + 32 * entry] = upper[entry]


def far_kernel(
    partner, count, own, inner, outer, coupling, low_table, upper, sums, out, prepared, extended
):
    top_sums(low_table, upper, sums, prepared)
    device = place_of_device()[0]
    odd = (device & 1) == 1
    extended[0:LOCAL] = jnp.where(odd, inner[0:LOCAL], outer[0:LOCAL])
    extended[LOCAL : 2 * LOCAL] = own[...]
    extended[2 * LOCAL : 3 * LOCAL] = jnp.where(odd, outer[0:LOCAL], inner[0:LOCAL])
    tables = [coupling[slot].reshape(LOCAL, 32, 128) for slot in range(SLOTS)]
    for clusters, offset in LAYOUT:
        for cluster in range(clusters):
            row = offset + cluster
            left = []
            right = []
            for slot in range(SLOTS):
                index = partner[slot, row]
                side = jnp.clip(index // clusters - device + 1, 0, 2)
                place = side * LOCAL + offset + index % clusters
                used = (slot < count[row]).astype(F32)
                left.append(coef_form(extended[place] * used))
                right.append(table_form(tables[slot][row]))
            out[row] = fold(dot(jnp.concatenate(left, axis=1), jnp.concatenate(right, axis=0)))


def call(kernel, name, outs, args, lazy=(), scalars=0, scratch=(), after=(), flops=0):
    vmem = pl.BlockSpec(memory_space=pltpu.VMEM)
    smem = pl.BlockSpec(memory_space=pltpu.SMEM)
    spare = pl.BlockSpec(memory_space=pl.ANY)
    given, slow, spares = len(args), len(lazy), len(after)
    parts = [(start, size) for _, start, size in lazy]
    lazy = [item for item, _, _ in lazy]

    def body(*refs):
        own = refs[given + slow + spares :]
        copies = []
        getters = []
        if slow:
            own, targets, semaphores = own[: -slow - 1], own[-slow - 1 : -1], own[-1]
            for i, target in enumerate(targets):
                source = refs[given + i].at[pl.ds(parts[i][0], parts[i][1])]
                copies.append(pltpu.make_async_copy(source, target, semaphores.at[i]))
                copies[-1].start()
            waiting = set(range(slow))

            def getter(i):
                def get():
                    if i in waiting:
                        waiting.remove(i)
                        copies[i].wait()
                    return targets[i]

                return get

            getters = [getter(i) for i in range(slow)]
        kernel(*refs[:given], *getters, *own)
        for get in getters:
            get()

    buffers = [
        pltpu.VMEM((size, *item.shape[1:]), item.dtype)
        for item, (_, size) in zip(lazy, parts)
    ]
    if lazy:
        buffers.append(pltpu.SemaphoreType.DMA((slow,)))
    result = pl.pallas_call(
        body,
        out_shape=list(outs),
        in_specs=[smem] * scalars + [vmem] * (given - scalars) + [spare] * (slow + spares),
        out_specs=[vmem] * len(outs),
        scratch_shapes=list(scratch) + buffers,
        compiler_params=pltpu.CompilerParams(
            vmem_limit_bytes=WIDE_BYTES if lazy else VMEM_BYTES
        ),
        cost_estimate=pl.CostEstimate(
            flops=flops, bytes_accessed=flops // 400, transcendentals=0
        ),
        name=name,
    )(*args, *lazy, *after)
    return result if len(result) > 1 else result[0]


def shape(*dims, dtype=F32):
    return jax.ShapeDtypeStruct(dims, dtype)


def permute(value, pairs):
    return lax.ppermute(value, "leaf", pairs)


def tables(size):
    return shape(size, 32, 128)


def prepare_kernel(transfers, couplings, group_raw, top_raw, group_pay):
    def coupling(level, side):
        return couplings[level - 1, :, side, :]

    group_pay[0] = coupling(GROUP_BITS, 1)
    top_raw[0:3] = transfers[4:7]
    top_raw[HIGH] = transfers[7]
    for side in range(2):
        for level in range(7, 10):
            top_raw[HIGH + 1 + 3 * side + level - 7] = coupling(level, side)
        for level in range(5, 7):
            top_raw[3 + 2 * side + level - 5] = coupling(level, side)
        for level in range(1, 5):
            group_raw[4 + 4 * side + level - 1] = coupling(level, side)
    group_raw[0:4] = transfers[0:4]


def choose(flag, first, second):
    return jnp.where(flag, first, second)


def merge_group(raw, bit, live, arrived, out):
    _, member, _ = place_of_device()
    right_child = ((member >> bit) & 1) == 1
    size = out.shape[0]
    start = 0
    if bit + 1 < GROUP_BITS:
        out[0] = choose(right_child, arrived[0], raw[bit + 1])
        start = 1
    for entry in range(start, size - 1):
        out[entry] = choose(right_child, arrived[entry], live[entry - start])
    out[size - 1] = choose(right_child, arrived[size - 1], raw[GROUP_BITS + bit])


def group_payload(raw, bit, live, pay):
    pay[0] = raw[bit + 1]
    size = live.shape[0]
    pay[1 : 1 + size] = live[...]
    pay[1 + size] = raw[2 * GROUP_BITS + bit]


def first_kernel(raw, arrived, top_raw, live, pay):
    merge_group(raw, 3, None, arrived, live)
    group_payload(raw, 2, live, pay)

    @pl.when(place_of_device()[1] == PORTER)
    def _():
        pay[0] = top_raw[HIGH + 6]
        pay[1] = top_raw[HIGH]


def second_kernel(raw, arrived, live, top_raw, out, pay, ninth):
    merge_group(raw, 2, live, arrived, out)
    group_payload(raw, 1, out, pay)
    _, member, group = place_of_device()
    value = choose(((group >> 4) & 1) == 1, arrived[0], top_raw[HIGH + 3])
    ninth[0] = value
    ninth[1] = arrived[1]

    @pl.when(member == PORTER)
    def _():
        pay[0] = value
        pay[1] = top_raw[HIGH + 5]
        pay[2] = arrived[1]


def third_kernel(raw, arrived, live, top_raw, ninth, out, pay, upper, near_pay):
    merge_group(raw, 1, live, arrived, out)
    group_payload(raw, 0, out, pay)
    _, member, group = place_of_device()
    right_child = ((group >> 3) & 1) == 1
    upper[...] = jnp.zeros_like(upper)

    @pl.when((member == PORTER) & ((group & 7) == 0))
    def _():
        own = top_raw[HIGH]
        across = choose(right_child, arrived[0], ninth[0])
        upper[0] = times_t(times(ninth[1], across), own)
        upper[1] = times_t(times(arrived[2], across), own)
        upper[2] = choose(right_child, arrived[1], top_raw[HIGH + 2])

    upper[3] = top_raw[HIGH + 1]
    upper[4] = top_raw[HIGH + 4]
    near_pay[0:5] = upper[...]
    near_pay[5] = top_raw[2]
    near_pay[6] = top_raw[6]


def fourth_kernel(top_raw, upper, near_in, far_in, out, keep, low_pay):
    _, _, group = place_of_device()
    place = group & 7
    for entry in range(5):
        value = choose(
            place == 2, near_in[entry], choose(place == 6, far_in[entry], upper[entry])
        )
        out[entry] = value
        low_pay[4 + entry] = value
    second = ((group >> 1) & 1) == 1
    sixth = choose(second, near_in[5], top_raw[2])
    coupling = choose(second, near_in[6], top_raw[4])
    for target, side in ((keep, 3), (low_pay, 5)):
        target[0] = sixth
        target[1] = coupling
        target[2] = top_raw[1]
        target[3] = top_raw[side]
    keep[4] = top_raw[0]


def share_kernel(root, raw, live, arrived, blocks, table, chain):
    _, member, _ = place_of_device()
    merge_group(raw, 0, live, arrived, table)
    value = root[...]
    chain[0] = value
    for level in range(GROUP_BITS):
        value = times(value, raw[0] if level == 0 else table[level - 1])
        if level + 1 < GROUP_BITS:
            chain[level + 1] = value
    for other in range(GROUP):
        apart = member ^ other
        level = sum((apart >= (1 << bit)).astype(jnp.int32) for bit in range(1, GROUP_BITS))
        blocks[other, 0:8] = chain[level]
        blocks[other, 8:16] = value


def total_of(pieces):
    total = pieces[0]
    for piece in pieces[1:]:
        total = total + piece
    return total


def rise_kernel(given, keep, near_in, blocks, sibling, table, chain):
    _, member, group = place_of_device()
    place = group & 7
    odd = (place & 1) == 1
    for entry in range(4):
        table[entry] = choose(odd, near_in[entry], keep[entry])
    table[4] = keep[4]
    for level in range(GROUP_BITS):
        sibling[level] = total_of(
            [given[member ^ apart, 0:8] for apart in range(1 << level, 2 << level)]
        )
    value = total_of([given[other, 8:16] for other in range(GROUP)])
    chain[0] = value
    for level in range(3):
        value = times(value, table[4 - 2 * level])
        chain[level + 1] = value
    for other in range(8):
        apart = place ^ other
        level = sum((apart >= (1 << bit)).astype(jnp.int32) for bit in range(1, 3))
        blocks[other, 0:8] = chain[level]
        blocks[other, 8:16] = value


def fifth_kernel(upper, low_in, far_in, out):
    _, _, group = place_of_device()
    place = group & 7
    for entry in range(5):
        value = choose((place & 1) == 1, low_in[4 + entry], upper[entry])
        out[entry] = choose((place == 4) | (place == 5), far_in[entry], value)


def middle_kernel(given, blocks, sums):
    _, _, group = place_of_device()
    place = group & 7
    value = total_of([given[other, 8:16] for other in range(8)])
    for other in range(4):
        blocks[other] = value
    for level in range(3):
        sums[level] = total_of(
            [given[place ^ apart, 0:8] for apart in range(1 << level, 2 << level)]
        )


def turn_kernel(given, prepared, out):
    _, _, group = place_of_device()
    line = group >> 3
    left = [coef_form(given[line ^ apart]) for apart in (2, 3, 1)]
    right = [table_form(prepared[40 + 32 * entry : 72 + 32 * entry]) for entry in range(3)]
    value = fold(dot(jnp.concatenate(left, axis=1), jnp.concatenate(right, axis=0)))
    value = times_t(value, prepared[8:40]) + prepared[0:8]
    for other in range(GROUP):
        out[other] = value


def down_kernel(given, prepared, far, forms, basis, near, out):
    prepared = prepared()
    value = times_t(given[PORTER], prepared[8:40]) + prepared[0:8]
    parents = [value]
    forms, far = forms(), far()
    for clusters, offset in reversed(LAYOUT):
        following = []
        for parent in range(clusters // 2):
            first = offset + 2 * parent
            pair = jnp.concatenate([forms[first], forms[first + 1]], axis=0)
            raw = times_t_raw(row_form(parents[parent]), pair)
            following.append(weave(raw, 0) + far[first])
            following.append(weave(raw, 1) + far[first + 1])
        parents = following
    basis, near = basis(), near()
    for leaf in range(LEAVES):
        high, low = split(unpack(parents[leaf]))
        basis_high, basis_low = split(basis[leaf])
        both = dot(jnp.concatenate([high, low], axis=0), basis_high)
        place = slice(leaf * POINTS, (leaf + 1) * POINTS)
        out[:, place] = both[:16] + both[16:] + dot(high, basis_low) + near[16 * leaf : 16 * leaf + 16]


def on_device(
    sources,
    leaf_cluster_basis,
    local_transfer,
    far_coupling,
    far_partner,
    far_count,
    top_transfer,
    top_coupling,
    near_block,
    near_partner,
    near_count,
):
    count = lax.axis_size("leaf")
    forward = [(i, i + 1) for i in range(1, count - 1, 2)]

    def handed(value, period, first, second):
        return permute(value, [(i + first, i + second) for i in range(0, count, period)])

    transfers = top_transfer.reshape(TOP_BITS, 32, 128)
    couplings = top_coupling.reshape(TOP_BITS, 2, 32, 128).transpose(0, 2, 1, 3)
    raw, top_raw, pay = call(
        prepare_kernel,
        "top_tables",
        [tables(12), tables(14), tables(1)],
        [transfers, couplings],
        flops=1 << 30,
    )
    group_in = handed(pay, 16, 0, 8)
    top_raw = handed(top_raw, GROUP, 0, PORTER)

    coefs, root, forms = call(
        up_kernel,
        "upward",
        [
            shape(LOCAL, 8, 128),
            shape(8, 128),
            shape(LOCAL, 64, 128, dtype=BF16),
        ],
        [sources, leaf_cluster_basis, local_transfer],
        flops=2 << 30,
    )
    live, pay = call(
        first_kernel,
        "hand_down_1",
        [tables(1), tables(3)],
        [raw, group_in, top_raw],
        flops=1 << 29,
    )
    pairs = [(i, i + 4) for i in range(0, count, 8)]
    pairs += [(i + PORTER, (i ^ 256) + PORTER) for i in range(0, count, 128)]
    group_in = permute(pay, pairs)
    live, pay, ninth = call(
        second_kernel,
        "hand_down_2",
        [tables(3), tables(5), tables(2)],
        [raw, group_in, live, top_raw],
        after=[root],
        flops=1 << 29,
    )
    pairs = [(i, i + 2) for i in range(0, count, 4)]
    pairs += [(i + PORTER, (i ^ 128) + PORTER) for i in range(0, count, 128)]
    group_in = permute(pay, pairs)
    live, pay, upper, near_pay = call(
        third_kernel,
        "hand_down_3",
        [tables(5), tables(7), tables(5), tables(7)],
        [raw, group_in, live, top_raw, ninth],
        flops=1 << 29,
    )
    group_in = handed(pay, 2, 0, 1)
    near_in = handed(near_pay, 64, PORTER, 32 + PORTER)
    far_in = handed(upper, 128, PORTER, 96 + PORTER)
    upper, keep, low_pay = call(
        fourth_kernel,
        "hand_down_4",
        [tables(5), tables(5), tables(9)],
        [top_raw, upper, near_in, far_in],
        flops=1 << 29,
    )
    low_in = handed(low_pay, 32, PORTER, 16 + PORTER)
    pairs = [(i + 32 + PORTER, i + 64 + PORTER) for i in range(0, count, 128)]
    pairs += [(i + 96 + PORTER, i + 80 + PORTER) for i in range(0, count, 128)]
    far_in = permute(upper, pairs)
    shares, group_table = call(
        share_kernel,
        "group_shares",
        [shape(GROUP, 16, 128), tables(7)],
        [root, raw, live, group_in],
        scratch=[pltpu.VMEM((GROUP_BITS, 8, 128), F32)],
        after=[keep],
        flops=2 << 30,
    )
    in_group = [list(range(first, first + GROUP)) for first in range(0, count, GROUP)]
    in_column = [
        list(range(line + member, line + 128, GROUP))
        for line in range(0, count, 128)
        for member in range(GROUP)
    ]
    in_line = [list(range(first, count, 128)) for first in range(128)]
    given = lax.all_to_all(shares, "leaf", 0, 0, axis_index_groups=in_group)
    blocks, sibling, low_table = call(
        rise_kernel,
        "column_shares",
        [shape(8, 16, 128), shape(GROUP_BITS, 8, 128), tables(5)],
        [given, keep, low_in],
        scratch=[pltpu.VMEM((4, 8, 128), F32)],
        flops=2 << 30,
    )
    given = lax.all_to_all(blocks, "leaf", 0, 0, axis_index_groups=in_column)
    inner, outer = call(
        edge_kernel,
        "edges",
        [shape(LOCAL + 2 * REACH, 8, 128)] * 2,
        [sources, coefs],
        after=[blocks],
        flops=1 << 29,
    )
    inner = permute(inner, [(i, i ^ 1) for i in range(count)])
    outer = permute(outer, forward + [(second, first) for first, second in forward])
    blocks, sums = call(
        middle_kernel,
        "line_shares",
        [shape(4, 8, 128), shape(3, 8, 128)],
        [given],
        flops=1 << 30,
    )
    upper = call(
        fifth_kernel,
        "hand_down_5",
        [tables(5)],
        [upper, low_in, far_in],
        after=[blocks],
        flops=1 << 29,
    )
    given = lax.all_to_all(blocks, "leaf", 0, 0, axis_index_groups=in_line)

    near = call(
        near_kernel,
        "near_field",
        [shape(NEAR_ROWS + 40, 128)],
        [
            near_partner.T,
            near_count,
            sources,
            inner,
            outer,
            near_block,
            sibling,
            raw,
            group_table,
        ],
        scalars=2,
        scratch=[pltpu.VMEM((LEAVES + 2 * REACH, 16, POINTS), F32)],
        flops=2 << 30,
    )
    far, prepared = call(
        far_kernel,
        "far_field",
        [shape(LOCAL, 8, 128), shape(136, 128)],
        [
            far_partner.T,
            far_count,
            coefs,
            inner,
            outer,
            far_coupling.transpose(1, 0, 2),
            low_table,
            upper,
            sums,
        ],
        scalars=2,
        scratch=[pltpu.VMEM((3 * LOCAL, 8, 128), F32)],
        flops=2 << 30,
    )
    turned = call(
        turn_kernel,
        "top_turn",
        [shape(GROUP, 8, 128)],
        [given, prepared],
        flops=2 << 30,
    )
    given = lax.all_to_all(turned, "leaf", 0, 0, axis_index_groups=in_group)
    return call(
        down_kernel,
        "downward",
        [shape(16, LEAVES * POINTS)],
        [given],
        lazy=[
            (near, NEAR_ROWS, 40),
            (far, 0, LOCAL),
            (forms, 0, LOCAL),
            (leaf_cluster_basis, 0, LEAVES),
            (near, 0, NEAR_ROWS),
        ],
        flops=4 << 30,
    )


def solution(mesh):
    placed = (
        P(None, "leaf"),
        P("leaf", None, None),
        P("leaf", None),
        P("leaf", None, None),
        P("leaf", None),
        P("leaf"),
        P("leaf", None, None),
        P("leaf", None, None, None),
        P("leaf", None, None, None),
        P("leaf", None),
        P("leaf"),
    )
    return jax.shard_map(
        on_device, mesh=mesh, in_specs=placed, out_specs=P(None, "leaf"), check_vma=False
    )
```
